32 devices in a mesh: grp: 4 (over x, core), dev: 8 (over z, y).
Axes of the slice: x: 2, y: 2, z: 4, core: 2. Of those that a mesh axis runs over, the one named last changes fastest.
Arguments:
- tokens: bfloat16 [4096, 2048], P(('grp', 'dev')), may hold values from -6 to 6
- queries: bfloat16 [4096, 2048], P(('grp', 'dev')), may hold values from -7.5 to 7.5
- suffix_keys: bfloat16 [4096, 2048], P(('grp', 'dev')), may hold values from -6 to 6
- suffix_values: bfloat16 [4096, 2048], P(('grp', 'dev')), may hold values from -6 to 6
- prefix_keys: bfloat16 [4, 256, 2048], P('grp', 'dev'), may hold values from -6 to 6
- prefix_values: bfloat16 [4, 256, 2048], P('grp', 'dev'), may hold values from -6 to 6
- out_weight: bfloat16 [2048, 2048], replicated, may hold values from -0.125 to 0.125
- norm_gain: float32 [2048], replicated, may hold values from 0.1 to 1.9
- routes: int32 [4096, 6], P(('grp', 'dev')), may hold values from 0 to 15, all different within a row; in each aligned block of 128 rows (0 to 127, 128 to 255, ...) at most 64 rows name the same one
- route_weights: float32 [4096, 6], P(('grp', 'dev')), may hold values from 0.05 to 0.5
- gate_up_weight: bfloat16 [32, 2048, 1408], P(('grp', 'dev')), may hold values from -0.125 to 0.125
- down_weight: bfloat16 [32, 704, 2048], P(('grp', 'dev')), may hold values from -0.15625 to 0.15625
Outputs:
- attended: bfloat16 [4096, 2048], P(('grp', 'dev'))
- routed: bfloat16 [4096, 2048], P(('grp', 'dev'))
The draws below stay inside these ranges and needn't reach their ends.
Inputs may be any that keep to these rules, and one draw needn't show every extreme that they name: `routes`: each row names 6 different experts. Within the rows of one request (aligned blocks of 128 rows) no expert is named by more than 64 rows, and in some block one expert is named exactly 64 times.
All inputs are finite; a program needn't handle non-finite values.
Results may differ from the reference program's by a relative error of at most 0.019.
Values may be sent and summed in bfloat16 or wider, within the bound.
No kernel may reach another device: no remote copies, remote signals or barrier semaphores. Data moves between devices by JAX's collectives and lax.ppermute only.
A program may use at most 128 MiB of HBM per device.

```python
import math
import jax
import jax.numpy as jnp
import numpy as np
from jax import lax

D = 2048
HEADS = 16
HEAD_DIM = 128
FF = 1408
TOP = 6
TOK_DEV = 128
EXPERTS = 16
HALF = 704
CAP = 64
PREFIX = 256
GROUPS = 4
TOKENS = 4096


def draw_queries(key, part):
    inner = jax.random.fold_in(key, 17)
    values = jnp.clip(1.5 * jax.random.normal(inner, (TOKENS, D), jnp.float32), -7.5, 7.5)
    return values.astype(jnp.bfloat16)


def draw_prefix_keys(key, part):
    inner = jax.random.fold_in(key, 29)
    values = jnp.clip(jax.random.normal(inner, (GROUPS, PREFIX, D), jnp.float32), -6.0, 6.0)
    return values.astype(jnp.bfloat16)


def level_of(rng, dims, split, least, top_value):
    factor_of = 1.0
    for axis_at, parts in split:
        heights = jax.random.uniform(jax.random.fold_in(jax.random.fold_in(rng, 6), axis_at), (parts,), jnp.float32, least / len(split), top_value / len(split))
        factor_of = factor_of * jnp.repeat(jnp.exp(heights), dims[axis_at] // parts).reshape((-1,) + (1,) * (len(dims) - 1 - axis_at))
    return factor_of


def shared_out(own_key, own, number, rows, amount, top, reach, lean):
    order = jax.random.permutation(own_key, amount)
    packed, ordinary = load_shares(amount, rows * top, reach, lean, True), load_shares(amount, rows * top, reach, lean, False)
    places = jnp.arange(amount)

    def named(tallies, rotation):
        used = int((tallies > 0).sum())
        fixed = max(1, used // 4)
        moved = fixed + (places - fixed + rotation * (used - fixed)) % max(1, amount - fixed)
        return jnp.zeros((amount,), jnp.int32).at[order[jnp.where(places < fixed, places, moved)]].set(jnp.asarray(tallies, jnp.int32))

    tallies = jnp.where(number % 4 == 0, named(packed, number // 4), named(ordinary, number - number // 4 - 1))
    mixed = jax.random.permutation(jax.random.fold_in(own, 3), amount)
    donor, receiver = mixed[0:amount // 2 * 2:2], mixed[1:amount // 2 * 2:2]
    slack = jnp.minimum(tallies[donor] - 1, reach - tallies[receiver]) // 2
    slack = jnp.where((donor == order[0]) | (receiver == order[0]) | (tallies[receiver] == 0), 0, jnp.maximum(slack, 0))
    moved = jax.random.randint(jax.random.fold_in(own, 4), (amount // 2,), 0, 1 << 20) % (slack + 1)
    tallies = tallies.at[donor].add(-moved).at[receiver].add(moved)
    members = jnp.searchsorted(jnp.cumsum(tallies), jnp.arange(rows * top), side="right").astype(jnp.int32)
    table = members.reshape(top, rows).T
    table = table[jax.random.permutation(jax.random.fold_in(own, 1), rows)]
    rotation = jax.random.randint(jax.random.fold_in(own, 2), (rows, 1), 0, top)
    return jnp.take_along_axis(table, (jnp.arange(top)[None, :] + rotation) % top, axis=1)


def load_shares(count, total, reach, skew, full):
    weights = [(1 << 20) // math.isqrt(standing ** skew) + 1 for standing in range(1, count + 1)]
    largest = reach if full else min(reach, max(-(-total // count), total * weights[0] // sum(weights)))
    least = 1 if total - largest >= count - 1 else 0
    holding, spare = [largest] + [least] * (count - 1), total - largest - least * (count - 1)
    while spare > 0:
        free = [i for i in range(1, count) if holding[i] < largest] or [i for i in range(1, count) if holding[i] < reach]
        mass, budget = sum([weights[i] for i in free]), spare
        for i in free:
            extra = min(reach - holding[i], max(1, budget * weights[i] // mass), spare)
            holding[i] = holding[i] + extra
            spare = spare - extra
    return np.array(holding)


def gaussian(own_key, dims, width, most, cuts=(), held_as=jnp.bfloat16):
    level = level_of(own_key, dims, cuts, -0.22, 0.18) if cuts else 1.0
    drawn = jax.random.normal(own_key, dims, jnp.float32) * width * level
    return jnp.minimum(jnp.maximum(drawn, -most), most).astype(held_as)


def setup_inputs(seed: int = 0) -> dict:
    key_of = jax.random.split(jax.random.key(seed), 13)
    tokens = gaussian(key_of[0], (TOKENS, D), 1.0, 6.0, ((0, 32),))
    queries = draw_queries(jax.random.fold_in(key_of[12], 71), 0)
    suffix_keys = gaussian(key_of[2], (TOKENS, D), 1.0, 6.0, ((0, 32),))
    suffix_values = gaussian(key_of[3], (TOKENS, D), 1.0, 6.0, ((0, 32),))
    prefix_keys = draw_prefix_keys(jax.random.fold_in(key_of[12], 71), 0)
    prefix_values = gaussian(key_of[5], (GROUPS, PREFIX, D), 1.0, 6.0, ((0, 4), (1, 8)))
    out_weight = gaussian(key_of[6], (D, D), D ** -0.5, 0.125)
    norm_gain = jnp.clip(1.0 + 0.18 * jax.random.normal(key_of[7], (D,), jnp.float32), 0.1, 1.9)
    routes_keys = jax.random.split(jax.random.fold_in(key_of[8], 1), TOKENS // TOK_DEV)
    routes_turns = jax.random.permutation(jax.random.fold_in(key_of[8], 3), TOKENS // TOK_DEV)
    routes = jax.vmap(lambda own, number: shared_out(jax.random.fold_in(key_of[8], 2), own, number, TOK_DEV, EXPERTS, TOP, CAP, 2))(routes_keys, routes_turns).reshape((TOKENS, TOP))
    route_weights = jnp.clip(jnp.exp(math.log(0.5) - 2.3025851 * jax.random.uniform(key_of[9], (TOKENS, TOP), jnp.float32) ** level_of(key_of[9], (TOKENS, TOP), ((0, 32),), -0.2, 0.2)), 0.05, 0.5)
    gate_up_weight = gaussian(key_of[10], (2 * EXPERTS, D, 2 * HALF), D ** -0.5, 0.125, ((0, 32),))
    down_weight = gaussian(key_of[11], (2 * EXPERTS, HALF, D), FF ** -0.5, 0.15625, ((0, 32),))
    return {"tokens": tokens, "queries": queries, "suffix_keys": suffix_keys, "suffix_values": suffix_values, "prefix_keys": prefix_keys, "prefix_values": prefix_values, "out_weight": out_weight, "norm_gain": norm_gain, "routes": routes, "route_weights": route_weights, "gate_up_weight": gate_up_weight, "down_weight": down_weight}


def half_expert(rows, gate_up, down_proj):
    hidden_units = down_proj.shape[0]
    projected = jnp.dot(rows, gate_up, preferred_element_type=jnp.float32)
    active = (jax.nn.silu(projected[:, :hidden_units]) * projected[:, hidden_units:]).astype(jnp.bfloat16)
    return jnp.dot(active, down_proj, preferred_element_type=jnp.float32).astype(jnp.bfloat16)

def attention_part(query_heads, key_rows, value_rows, allowed):
    key_heads = key_rows.astype(jnp.float32).reshape(-1, HEADS, HEAD_DIM)
    value_heads = value_rows.astype(jnp.float32).reshape(-1, HEADS, HEAD_DIM)
    scores = jnp.einsum('rhd,khd->hrk', query_heads, key_heads, precision=lax.Precision.HIGHEST) / math.sqrt(HEAD_DIM)
    scores = jnp.where(allowed[None], scores, -jnp.inf)
    row_max = lax.optimization_barrier(jnp.max(scores, axis=-1))
    shifted = jnp.exp(scores - row_max[..., None])
    row_sum = lax.optimization_barrier(jnp.sum(shifted, axis=-1))
    rounded = lax.optimization_barrier(shifted.astype(jnp.bfloat16)).astype(jnp.float32)
    weighted = jnp.einsum('hrk,khd->hrd', rounded, value_heads, precision=lax.Precision.HIGHEST)
    return (row_max, row_sum, weighted)

def reference(tokens, queries, suffix_keys, suffix_values, prefix_keys, prefix_values, out_weight, norm_gain, routes, route_weights, gate_up_weight, down_weight):
    requests_group = TOKENS // (TOK_DEV * GROUPS)
    causal = jnp.arange(TOK_DEV)[:, None] >= jnp.arange(TOK_DEV)[None, :]
    everything = jnp.ones((TOK_DEV, PREFIX), dtype=bool)

    def one_request(index):
        offset = (index * TOK_DEV).astype(jnp.int32)
        group = (index // requests_group).astype(jnp.int32)
        query_heads = lax.dynamic_slice_in_dim(queries, offset, TOK_DEV, 0).astype(jnp.float32).reshape(TOK_DEV, HEADS, HEAD_DIM)
        keys_before = lax.dynamic_index_in_dim(prefix_keys, group, 0, keepdims=False)
        values_before = lax.dynamic_index_in_dim(prefix_values, group, 0, keepdims=False)
        keys_after = lax.dynamic_slice_in_dim(suffix_keys, offset, TOK_DEV, 0)
        values_after = lax.dynamic_slice_in_dim(suffix_values, offset, TOK_DEV, 0)
        prefix_max, prefix_sum, prefix_acc = attention_part(query_heads, keys_before, values_before, everything)
        suffix_max, suffix_sum, suffix_acc = attention_part(query_heads, keys_after, values_after, causal)
        merged_max = jnp.maximum(prefix_max, suffix_max)
        prefix_scale = jnp.exp(prefix_max - merged_max)
        suffix_scale = jnp.exp(suffix_max - merged_max)
        mixed = (prefix_acc * prefix_scale[..., None] + suffix_acc * suffix_scale[..., None]) / (prefix_sum * prefix_scale + suffix_sum * suffix_scale)[..., None]
        heads_out = jnp.transpose(mixed, (1, 0, 2)).reshape(TOK_DEV, D).astype(jnp.bfloat16)
        return jnp.dot(heads_out, out_weight, preferred_element_type=jnp.float32).astype(jnp.bfloat16)
    attended = lax.map(one_request, jnp.arange(TOKENS // TOK_DEV, dtype=jnp.int32)).reshape(TOKENS, D)
    residual = tokens.astype(jnp.float32) + attended.astype(jnp.float32)
    mean_square = lax.optimization_barrier(jnp.mean(residual * residual, axis=-1, keepdims=True))
    normed = (residual * lax.rsqrt(mean_square + 1e-06) * norm_gain).astype(jnp.bfloat16)
    blocks = TOKENS // TOK_DEV
    flat_routes = routes.reshape(blocks, TOK_DEV * TOP)
    onehot = (flat_routes[..., None] == jnp.arange(EXPERTS, dtype=jnp.int32)).astype(jnp.int32)
    ranking = lax.optimization_barrier(jnp.sum(jnp.cumsum(onehot, axis=1) * onehot, axis=-1)) - 1
    slots = flat_routes * CAP + ranking
    owners = (jnp.arange(TOKENS * TOP, dtype=jnp.int32) // TOP).reshape(blocks, TOK_DEV * TOP)
    block_rows = jnp.arange(blocks, dtype=jnp.int32)[:, None]
    owner_table = jnp.full((blocks, EXPERTS * CAP), TOKENS, jnp.int32).at[block_rows, slots].set(owners)
    weight_table = jnp.zeros((blocks, EXPERTS * CAP), jnp.float32).at[block_rows, slots].set(route_weights.reshape(blocks, TOK_DEV * TOP))

    def expert_step(routed_sum, expert):
        begin = (expert * CAP).astype(jnp.int32)
        picked = lax.dynamic_slice_in_dim(owner_table, begin, CAP, 1).reshape(-1)
        gates = lax.dynamic_slice_in_dim(weight_table, begin, CAP, 1).reshape(-1)
        rows = jnp.take(normed, picked, axis=0, mode='fill', fill_value=0)
        first = half_expert(rows, lax.dynamic_index_in_dim(gate_up_weight, (2 * expert).astype(jnp.int32), 0, keepdims=False), lax.dynamic_index_in_dim(down_weight, (2 * expert).astype(jnp.int32), 0, keepdims=False))
        second = half_expert(rows, lax.dynamic_index_in_dim(gate_up_weight, (2 * expert + 1).astype(jnp.int32), 0, keepdims=False), lax.dynamic_index_in_dim(down_weight, (2 * expert + 1).astype(jnp.int32), 0, keepdims=False))
        output = lax.optimization_barrier((first.astype(jnp.float32) + second.astype(jnp.float32)).astype(jnp.bfloat16)).astype(jnp.float32)
        routed_sum = routed_sum.at[picked].add(output * gates[:, None], mode='drop')
        return (routed_sum, None)
    routed_sum, unused = lax.scan(expert_step, jnp.zeros((TOKENS, D), jnp.float32), jnp.arange(EXPERTS, dtype=jnp.int32))
    return (attended, routed_sum.astype(jnp.bfloat16))
```

```python
import math

import jax
import jax.numpy as jnp
from jax import lax
from jax.experimental import pallas as pl
from jax.experimental.pallas import tpu as pltpu
from jax.sharding import PartitionSpec as P

HEADS = 16
HEAD_DIM = 128
TOP = 6
GATHER_BUDGET = 40 * 2**20
VMEM_LIMIT = 52 * 2**20


def attention_kernel(q_ref, kv_ref, sk_ref, sv_ref, out_ref):
    rows = q_ref.shape[0]
    span = q_ref.shape[1]
    scale = 1.0 / math.sqrt(HEAD_DIM)
    causal = lax.broadcasted_iota(jnp.int32, (rows, rows), 0) >= lax.broadcasted_iota(
        jnp.int32, (rows, rows), 1
    )
    contract = (((1,), (1,)), ((), ()))
    for head in range(span // HEAD_DIM):
        cols = slice(head * HEAD_DIM, (head + 1) * HEAD_DIM)
        query = q_ref[:, cols]
        keys = kv_ref[:, 0, :, cols].reshape(-1, HEAD_DIM)
        values = kv_ref[:, 1, :, cols].reshape(-1, HEAD_DIM)
        prefix = (
            lax.dot_general(query, keys, contract, preferred_element_type=jnp.float32) * scale
        )
        suffix = (
            lax.dot_general(query, sk_ref[:, cols], contract, preferred_element_type=jnp.float32)
            * scale
        )
        suffix = jnp.where(causal, suffix, -jnp.inf)
        top = jnp.maximum(
            jnp.max(prefix, axis=1, keepdims=True), jnp.max(suffix, axis=1, keepdims=True)
        )
        prefix = jnp.exp(prefix - top)
        suffix = jnp.exp(suffix - top)
        total = jnp.sum(prefix, axis=1, keepdims=True) + jnp.sum(suffix, axis=1, keepdims=True)
        mixed = jnp.dot(
            prefix.astype(jnp.bfloat16), values, preferred_element_type=jnp.float32
        ) + jnp.dot(
            suffix.astype(jnp.bfloat16), sv_ref[:, cols], preferred_element_type=jnp.float32
        )
        out_ref[:, cols] = (mixed / total).astype(jnp.bfloat16)


def attention(queries, kv, suffix_keys, suffix_values):
    rows, width = queries.shape
    span = 4 * HEAD_DIM
    by_cols = pl.BlockSpec((rows, span), lambda i: (0, i))
    return pl.pallas_call(
        attention_kernel,
        grid=(width // span,),
        in_specs=[
            by_cols,
            pl.BlockSpec(kv.shape[:3] + (span,), lambda i: (0, 0, 0, i)),
            by_cols,
            by_cols,
        ],
        out_specs=by_cols,
        out_shape=jax.ShapeDtypeStruct((rows, width), jnp.bfloat16),
        compiler_params=pltpu.CompilerParams(vmem_limit_bytes=VMEM_LIMIT),
        name="attention",
    )(queries, kv, suffix_keys, suffix_values)


def project_kernel(heads_ref, weight_ref, tokens_ref, gain_ref, attended_ref, normed_ref, held):
    step = pl.program_id(0)
    attended = jnp.dot(
        heads_ref[...], weight_ref[...], preferred_element_type=jnp.float32
    ).astype(jnp.bfloat16)
    attended_ref[...] = attended
    held[step] = tokens_ref[...].astype(jnp.float32) + attended.astype(jnp.float32)

    @pl.when(step == pl.num_programs(0) - 1)
    def finish():
        steps, rows, span = held.shape
        squares = jnp.zeros((rows, 1), jnp.float32)
        for piece in range(steps):
            part = held[piece]
            squares = squares + jnp.sum(part * part, axis=1, keepdims=True)
        factor = lax.rsqrt(squares / (steps * span) + 1e-06)
        for piece in range(steps):
            cols = slice(piece * span, (piece + 1) * span)
            normed_ref[:, cols] = (held[piece] * factor * gain_ref[:, cols]).astype(jnp.bfloat16)


def project(heads_out, out_weight, tokens, norm_gain):
    rows, width = tokens.shape
    span = 512
    steps = width // span
    by_cols = pl.BlockSpec((rows, span), lambda i: (0, i))
    return pl.pallas_call(
        project_kernel,
        grid=(steps,),
        in_specs=[
            pl.BlockSpec((rows, width), lambda i: (0, 0)),
            pl.BlockSpec((width, span), lambda i: (0, i)),
            by_cols,
            pl.BlockSpec((1, width), lambda i: (0, 0)),
        ],
        out_specs=[by_cols, pl.BlockSpec((rows, width), lambda i: (0, 0))],
        out_shape=[
            jax.ShapeDtypeStruct((rows, width), jnp.bfloat16),
            jax.ShapeDtypeStruct((rows, width), jnp.bfloat16),
        ],
        scratch_shapes=[pltpu.VMEM((steps, rows, span), jnp.float32)],
        compiler_params=pltpu.CompilerParams(vmem_limit_bytes=VMEM_LIMIT),
        name="project_and_norm",
    )(heads_out, out_weight, tokens, norm_gain.reshape(1, width))


def expert_kernel(
    capacity, rows_ref, slot_ref, gate_ref, gate_up_ref, down_ref, out_ref, picked, weighted
):
    requests, _, rows = slot_ref.shape
    hidden = down_ref.shape[0]
    levels = lax.broadcasted_iota(jnp.int32, (capacity, rows), 0)
    for one in range(requests):
        chosen = levels == slot_ref[one]
        picked[one * capacity : (one + 1) * capacity, :] = jnp.dot(
            chosen.astype(jnp.bfloat16),
            rows_ref[one * rows : (one + 1) * rows, :],
            preferred_element_type=jnp.float32,
        ).astype(jnp.bfloat16)
    projected = jnp.dot(picked[...], gate_up_ref[...], preferred_element_type=jnp.float32)
    gate = projected[:, :hidden]
    active = (gate / (1.0 + jnp.exp(-gate)) * projected[:, hidden:]).astype(jnp.bfloat16)
    weighted[...] = jnp.dot(active, down_ref[...], preferred_element_type=jnp.float32)
    for one in range(requests):
        chosen = levels == slot_ref[one]
        gates = jnp.sum(jnp.where(chosen, gate_ref[one], 0.0), axis=1, keepdims=True)
        scaled = (weighted[one * capacity : (one + 1) * capacity, :] * gates).astype(jnp.bfloat16)
        out_ref[one * rows : (one + 1) * rows, :] = lax.dot_general(
            chosen.astype(jnp.bfloat16),
            scaled,
            (((0,), (0,)), ((), ())),
            preferred_element_type=jnp.float32,
        ).astype(jnp.bfloat16)


def expert(gathered, slots, gates, gate_up, down, capacity):
    requests, rows = slots.shape
    width = gathered.shape[1]
    step = 4
    table = pl.BlockSpec((step, 1, rows), lambda i: (i, 0, 0))
    by_rows = pl.BlockSpec((step * rows, width), lambda i: (i, 0))
    return pl.pallas_call(
        lambda *refs: expert_kernel(capacity, *refs),
        grid=(requests // step,),
        in_specs=[
            by_rows,
            table,
            table,
            pl.BlockSpec(gate_up.shape, lambda i: (0, 0)),
            pl.BlockSpec(down.shape, lambda i: (0, 0)),
        ],
        out_specs=by_rows,
        out_shape=jax.ShapeDtypeStruct(gathered.shape, jnp.bfloat16),
        scratch_shapes=[
            pltpu.VMEM((step * capacity, width), jnp.bfloat16),
            pltpu.VMEM((step * capacity, width), jnp.float32),
        ],
        compiler_params=pltpu.CompilerParams(vmem_limit_bytes=VMEM_LIMIT),
        name="expert_half",
    )(
        gathered,
        slots.reshape(requests, 1, rows),
        gates.reshape(requests, 1, rows),
        gate_up,
        down,
    )


def half_expert(rows, gate_up, down_proj):
    hidden_units = down_proj.shape[0]
    projected = jnp.dot(rows, gate_up, preferred_element_type=jnp.float32)
    active = (jax.nn.silu(projected[:, :hidden_units]) * projected[:, hidden_units:]).astype(
        jnp.bfloat16
    )
    return jnp.dot(active, down_proj, preferred_element_type=jnp.float32).astype(jnp.bfloat16)


def exchange_plan(normed, routes, route_weights, gate_up, down, experts, capacity):
    rows_here, width = normed.shape
    flat_routes = routes.reshape(-1)
    onehot = (flat_routes[:, None] == jnp.arange(experts, dtype=jnp.int32)[None, :]).astype(
        jnp.int32
    )
    ranking = jnp.sum(jnp.cumsum(onehot, axis=0) * onehot, axis=1) - 1
    slots = flat_routes * capacity + ranking
    owners = jnp.arange(rows_here * TOP, dtype=jnp.int32) // TOP
    outgoing = jnp.zeros((experts * capacity, width), jnp.bfloat16).at[slots].set(normed[owners])
    buffer = jnp.broadcast_to(
        outgoing.reshape(experts, 1, capacity, width), (experts, 2, capacity, width)
    ).reshape(2 * experts, capacity, width)
    received = lax.all_to_all(buffer, ("grp", "dev"), split_axis=0, concat_axis=0, tiled=True)
    partial_rows = half_expert(received.reshape(-1, width), gate_up, down).reshape(
        2 * experts, capacity, width
    )
    returned = lax.all_to_all(partial_rows, ("grp", "dev"), split_axis=0, concat_axis=0, tiled=True)
    halves = returned.reshape(experts, 2, capacity, width)
    expert_table = lax.optimization_barrier(
        (halves[:, 0].astype(jnp.float32) + halves[:, 1].astype(jnp.float32)).astype(jnp.bfloat16)
    ).reshape(experts * capacity, width)
    picked = expert_table[slots].astype(jnp.float32)
    weighted_rows = picked * route_weights.reshape(-1)[:, None]
    return jnp.sum(weighted_rows.reshape(rows_here, TOP, width), axis=1).astype(jnp.bfloat16)


def own_slots(table, mine):
    named = table[:, :TOP] == mine.astype(jnp.float32)
    gates = jnp.sum(jnp.where(named, table[:, TOP:], 0.0), axis=1)
    member = jnp.any(named, axis=1)
    rows = table.shape[-1]
    before = jnp.arange(rows)[:, None] <= jnp.arange(rows)[None, :]
    ranks = jnp.dot(
        member.astype(jnp.bfloat16),
        before.astype(jnp.bfloat16),
        preferred_element_type=jnp.float32,
    ).astype(jnp.int32)
    return jnp.where(member, ranks - 1, -1), gates


def gather_plan(normed, table, gate_up, down, experts, capacity):
    mine = (lax.axis_index("grp") * lax.axis_size("dev") + lax.axis_index("dev")) // 2
    slots, gates = own_slots(table, mine)
    gathered = lax.all_gather(normed, ("grp", "dev"), axis=0, tiled=True)
    partial = expert(gathered, slots, gates, gate_up, down, capacity)
    return lax.psum_scatter(partial, ("grp", "dev"), scatter_dimension=0, tiled=True)


def on_device(
    tokens,
    queries,
    suffix_keys,
    suffix_values,
    prefix_keys,
    prefix_values,
    out_weight,
    norm_gain,
    routes,
    route_weights,
    gate_up_weight,
    down_weight,
):
    rows_here, width = tokens.shape
    groups = lax.axis_size("grp")
    members = lax.axis_size("dev")
    experts = groups * members // 2
    capacity = 4 * rows_here * TOP // (3 * experts)
    gather_fits = groups * members * rows_here * width * 2 <= GATHER_BUDGET
    kv = lax.all_gather(jnp.concatenate([prefix_keys, prefix_values]), "dev", axis=0)
    if gather_fits:
        table = lax.all_gather(
            jnp.concatenate([routes.T.astype(jnp.float32), route_weights.T]),
            ("grp", "dev"),
            axis=0,
        )
    heads_out = attention(queries, kv, suffix_keys, suffix_values)
    attended, normed = project(heads_out, out_weight, tokens, norm_gain)
    if gather_fits:
        routed = gather_plan(normed, table, gate_up_weight[0], down_weight[0], experts, capacity)
    else:
        routed = exchange_plan(
            normed, routes, route_weights, gate_up_weight[0], down_weight[0], experts, capacity
        )
    return (attended, routed)


def solution(mesh):
    return jax.shard_map(
        on_device,
        mesh=mesh,
        in_specs=(
            P(("grp", "dev"), None),
            P(("grp", "dev"), None),
            P(("grp", "dev"), None),
            P(("grp", "dev"), None),
            P("grp", "dev", None),
            P("grp", "dev", None),
            P(),
            P(),
            P(("grp", "dev"), None),
            P(("grp", "dev"), None),
            P(("grp", "dev"), None, None),
            P(("grp", "dev"), None, None),
        ),
        out_specs=(P(("grp", "dev"), None), P(("grp", "dev"), None)),
        check_vma=False,
    )
```

```python
import math

import jax
import jax.numpy as jnp
from jax import lax
from jax.experimental import pallas as pl
from jax.experimental.pallas import tpu as pltpu
from jax.sharding import Mesh
from jax.sharding import PartitionSpec as P

HEADS = 16
HEAD_DIM = 128
TOP = 6
ALL = ("far", "core", "line", "side")
GATHER_BUDGET = 40 * 2**20
VMEM_LIMIT = 52 * 2**20


def attention_kernel(q_ref, sk_ref, sv_ref, *refs):
    pieces, out_ref = refs[:-1], refs[-1]
    rows = q_ref.shape[0]
    span = q_ref.shape[1]
    scale = 1.0 / math.sqrt(HEAD_DIM)
    causal = lax.broadcasted_iota(jnp.int32, (rows, rows), 0) >= lax.broadcasted_iota(
        jnp.int32, (rows, rows), 1
    )
    contract = (((1,), (1,)), ((), ()))
    for head in range(span // HEAD_DIM):
        cols = slice(head * HEAD_DIM, (head + 1) * HEAD_DIM)
        query = q_ref[:, cols]
        keys = jnp.concatenate([piece[0, :, cols] for piece in pieces])
        values = jnp.concatenate([piece[1, :, cols] for piece in pieces])
        prefix = (
            lax.dot_general(query, keys, contract, preferred_element_type=jnp.float32) * scale
        )
        suffix = (
            lax.dot_general(query, sk_ref[:, cols], contract, preferred_element_type=jnp.float32)
            * scale
        )
        suffix = jnp.where(causal, suffix, -jnp.inf)
        top = jnp.maximum(
            jnp.max(prefix, axis=1, keepdims=True), jnp.max(suffix, axis=1, keepdims=True)
        )
        prefix = jnp.exp(prefix - top)
        suffix = jnp.exp(suffix - top)
        total = jnp.sum(prefix, axis=1, keepdims=True) + jnp.sum(suffix, axis=1, keepdims=True)
        mixed = jnp.dot(
            prefix.astype(jnp.bfloat16), values, preferred_element_type=jnp.float32
        ) + jnp.dot(
            suffix.astype(jnp.bfloat16), sv_ref[:, cols], preferred_element_type=jnp.float32
        )
        out_ref[:, cols] = (mixed / total).astype(jnp.bfloat16)


def attention(queries, suffix_keys, suffix_values, pieces):
    rows, width = queries.shape
    span = 4 * HEAD_DIM
    by_cols = pl.BlockSpec((rows, span), lambda i: (0, i))
    return pl.pallas_call(
        attention_kernel,
        grid=(width // span,),
        in_specs=[by_cols] * 3
        + [pl.BlockSpec(piece.shape[:2] + (span,), lambda i: (0, 0, i)) for piece in pieces],
        out_specs=by_cols,
        out_shape=jax.ShapeDtypeStruct((rows, width), jnp.bfloat16),
        compiler_params=pltpu.CompilerParams(vmem_limit_bytes=VMEM_LIMIT),
        name="attention",
    )(queries, suffix_keys, suffix_values, *pieces)


def project_kernel(heads_ref, weight_ref, tokens_ref, gain_ref, attended_ref, normed_ref, held):
    step = pl.program_id(0)
    attended = jnp.dot(
        heads_ref[...], weight_ref[...], preferred_element_type=jnp.float32
    ).astype(jnp.bfloat16)
    attended_ref[...] = attended
    held[step] = tokens_ref[...].astype(jnp.float32) + attended.astype(jnp.float32)

    @pl.when(step == pl.num_programs(0) - 1)
    def finish():
        steps, rows, span = held.shape
        squares = jnp.zeros((rows, 1), jnp.float32)
        for piece in range(steps):
            part = held[piece]
            squares = squares + jnp.sum(part * part, axis=1, keepdims=True)
        factor = lax.rsqrt(squares / (steps * span) + 1e-06)
        for piece in range(steps):
            cols = slice(piece * span, (piece + 1) * span)
            normed_ref[:, cols] = (held[piece] * factor * gain_ref[:, cols]).astype(jnp.bfloat16)


def project(heads_out, out_weight, tokens, norm_gain):
    rows, width = tokens.shape
    span = 512
    steps = width // span
    by_cols = pl.BlockSpec((rows, span), lambda i: (0, i))
    return pl.pallas_call(
        project_kernel,
        grid=(steps,),
        in_specs=[
            pl.BlockSpec((rows, width), lambda i: (0, 0)),
            pl.BlockSpec((width, span), lambda i: (0, i)),
            by_cols,
            pl.BlockSpec((1, width), lambda i: (0, 0)),
        ],
        out_specs=[by_cols, pl.BlockSpec((rows, width), lambda i: (0, 0))],
        out_shape=[
            jax.ShapeDtypeStruct((rows, width), jnp.bfloat16),
            jax.ShapeDtypeStruct((rows, width), jnp.bfloat16),
        ],
        scratch_shapes=[pltpu.VMEM((steps, rows, span), jnp.float32)],
        compiler_params=pltpu.CompilerParams(vmem_limit_bytes=VMEM_LIMIT),
        name="project_and_norm",
    )(heads_out, out_weight, tokens, norm_gain.reshape(1, width))


def experts_kernel(
    capacity,
    place_ref,
    rows_ref,
    slot_ref,
    gate_ref,
    own_up_ref,
    own_down_ref,
    other_up_ref,
    other_down_ref,
    first_ref,
    second_ref,
    picked,
    scaled,
):
    requests = rows_ref.shape[1]
    rows = rows_ref.shape[3]
    hidden = own_down_ref.shape[0]
    half = first_ref.shape[2]
    levels = lax.broadcasted_iota(jnp.int32, (2 * capacity, rows), 0)
    for one in range(requests):
        chosen = (levels == slot_ref[0, one, 0, 0]) | (levels == slot_ref[0, one, 0, 1])
        taken = jnp.dot(
            chosen.astype(jnp.bfloat16), rows_ref[0, one, 0], preferred_element_type=jnp.float32
        ).astype(jnp.bfloat16)
        picked[0, one * capacity : (one + 1) * capacity, :] = taken[:capacity]
        picked[1, one * capacity : (one + 1) * capacity, :] = taken[capacity:]
    for which, (up_ref, down_ref) in enumerate(
        [(own_up_ref, own_down_ref), (other_up_ref, other_down_ref)]
    ):
        projected = jnp.dot(picked[which], up_ref[...], preferred_element_type=jnp.float32)
        gate = projected[:, :hidden]
        active = (gate / (1.0 + jnp.exp(-gate)) * projected[:, hidden:]).astype(jnp.bfloat16)
        result = jnp.dot(active, down_ref[...], preferred_element_type=jnp.float32)
        for one in range(requests):
            low = which * capacity
            chosen = levels[low : low + capacity] == slot_ref[0, one, 0, which]
            gates = jnp.sum(
                jnp.where(chosen, gate_ref[0, one, 0, which], 0.0), axis=1, keepdims=True
            )
            scaled[one, low : low + capacity, :] = (
                result[one * capacity : (one + 1) * capacity, :] * gates
            ).astype(jnp.bfloat16)
    for one in range(requests):
        chosen = (levels == slot_ref[0, one, 0, 0]) | (levels == slot_ref[0, one, 0, 1])
        summed = lax.dot_general(
            chosen.astype(jnp.bfloat16),
            scaled[one],
            (((0,), (0,)), ((), ())),
            preferred_element_type=jnp.float32,
        ).astype(jnp.bfloat16)
        first_ref[0, one * rows : (one + 1) * rows, :] = summed[:, :half]
        second_ref[0, one * rows : (one + 1) * rows, :] = summed[:, half:]


def run_experts(gathered, slots, gates, weights, offsets, capacity):
    layers, requests, _, rows, width = gathered.shape
    steps = offsets.shape[0]
    half = width // 2
    blocks = lambda i, place: (place[i, 0], 0, place[i, 1], 0, 0)
    table = pl.BlockSpec((1, requests, 1, 2, 1, rows), lambda i, place: blocks(i, place) + (0,))
    whole = [
        pl.BlockSpec(one.shape, lambda i, place: (0, 0), pipeline_mode=pl.Buffered(1))
        for one in weights
    ]
    part = pl.BlockSpec((1, requests * rows, half), lambda i, place: (i, 0, 0))
    slots_in_step = 2 * requests * capacity
    hidden = weights[1].shape[0]
    return pl.pallas_call(
        lambda *refs: experts_kernel(capacity, *refs),
        grid_spec=pltpu.PrefetchScalarGridSpec(
            num_scalar_prefetch=1,
            grid=(steps,),
            in_specs=[pl.BlockSpec((1, requests, 1, rows, width), blocks), table, table] + whole,
            out_specs=[part, part],
            scratch_shapes=[
                pltpu.VMEM((2, requests * capacity, width), jnp.bfloat16),
                pltpu.VMEM((requests, 2 * capacity, width), jnp.bfloat16),
            ],
        ),
        out_shape=[jax.ShapeDtypeStruct((steps, requests * rows, half), jnp.bfloat16)] * 2,
        compiler_params=pltpu.CompilerParams(vmem_limit_bytes=VMEM_LIMIT),
        cost_estimate=pl.CostEstimate(
            flops=steps * slots_in_step * width * hidden * 6,
            bytes_accessed=sum(one.size * 2 for one in weights)
            + steps * requests * rows * width * 4,
            transcendentals=steps * slots_in_step * hidden,
        ),
        name="experts",
    )(offsets, gathered, slots, gates, *weights)


def half_expert(rows, gate_up, down_proj):
    hidden_units = down_proj.shape[0]
    projected = jnp.dot(rows, gate_up, preferred_element_type=jnp.float32)
    active = (jax.nn.silu(projected[:, :hidden_units]) * projected[:, hidden_units:]).astype(
        jnp.bfloat16
    )
    return jnp.dot(active, down_proj, preferred_element_type=jnp.float32).astype(jnp.bfloat16)


def exchange_plan(normed, routes, route_weights, gate_up, down, experts, capacity):
    rows_here, width = normed.shape
    flat_routes = routes.reshape(-1)
    onehot = (flat_routes[:, None] == jnp.arange(experts, dtype=jnp.int32)[None, :]).astype(
        jnp.int32
    )
    ranking = jnp.sum(jnp.cumsum(onehot, axis=0) * onehot, axis=1) - 1
    slots = flat_routes * capacity + ranking
    owners = jnp.arange(rows_here * TOP, dtype=jnp.int32) // TOP
    outgoing = jnp.zeros((experts * capacity, width), jnp.bfloat16).at[slots].set(normed[owners])
    buffer = jnp.broadcast_to(
        outgoing.reshape(experts, 1, capacity, width), (experts, 2, capacity, width)
    ).reshape(2 * experts, capacity, width)
    received = lax.all_to_all(buffer, ALL, split_axis=0, concat_axis=0, tiled=True)
    partial_rows = half_expert(received.reshape(-1, width), gate_up, down).reshape(
        2 * experts, capacity, width
    )
    returned = lax.all_to_all(partial_rows, ALL, split_axis=0, concat_axis=0, tiled=True)
    halves = returned.reshape(experts, 2, capacity, width)
    expert_table = lax.optimization_barrier(
        (halves[:, 0].astype(jnp.float32) + halves[:, 1].astype(jnp.float32)).astype(jnp.bfloat16)
    ).reshape(experts * capacity, width)
    picked = expert_table[slots].astype(jnp.float32)
    weighted_rows = picked * route_weights.reshape(-1)[:, None]
    return jnp.sum(weighted_rows.reshape(rows_here, TOP, width), axis=1).astype(jnp.bfloat16)


def own_slots(table, mine, first_slot):
    named = table[:, :TOP] == mine.astype(jnp.float32)
    gates = jnp.sum(jnp.where(named, table[:, TOP:], 0.0), axis=1)
    member = jnp.any(named, axis=1)
    rows = table.shape[-1]
    before = jnp.arange(rows)[:, None] <= jnp.arange(rows)[None, :]
    ranks = jnp.dot(
        member.astype(jnp.bfloat16),
        before.astype(jnp.bfloat16),
        preferred_element_type=jnp.float32,
    ).astype(jnp.int32)
    return jnp.where(member, ranks - 1 + first_slot, -1), gates


def swap(array, axis):
    return lax.ppermute(array, axis, [(0, 1), (1, 0)])


def shift(array, axis, amount):
    size = lax.axis_size(axis)
    return lax.ppermute(array, axis, [(i, (i + amount) % size) for i in range(size)])


def add(*arrays):
    return sum(one.astype(jnp.float32) for one in arrays).astype(jnp.bfloat16)


def gather_plan(normed, table, weights, capacity):
    rows, width = normed.shape
    layers, columns = lax.axis_size("far"), lax.axis_size("line")
    far, core = lax.axis_index("far"), lax.axis_index("core")
    line, side = lax.axis_index("line"), lax.axis_index("side")
    own = (far * 2 + core) * columns + line
    other = (far * 2 + 1 - core) * columns + line
    own_slot, own_gate = own_slots(table, own, 0)
    other_slot, other_gate = own_slots(table, other, capacity)
    shape = (layers, columns, 2, 2, 1, rows)
    slots = jnp.stack([own_slot, other_slot], axis=1).reshape(shape)
    gates = jnp.stack([own_gate, other_gate], axis=1).reshape(shape)
    gathered = lax.all_gather(normed, ("far", "line", "side"), axis=0).reshape(
        layers, columns, 2, rows, width
    )
    place = lambda a, b: jnp.stack([far ^ a, side ^ b])
    first = run_experts(
        gathered, slots, gates, weights, jnp.stack([place(1, 1)]).astype(jnp.int32), capacity
    )
    rest = run_experts(
        gathered,
        slots,
        gates,
        weights,
        jnp.stack([place(0, 1), place(1, 0), place(0, 0)]).astype(jnp.int32),
        capacity,
    )
    a_corner = swap(first[0][0], "side")
    b_corner = swap(first[1][0], "far")
    a_side = swap(rest[0][0], "side")
    b_far = swap(rest[1][1], "far")
    a_far = swap(add(rest[0][1], a_corner), "far")
    b_side = swap(add(rest[1][0], b_corner), "side")
    total = jnp.concatenate(
        [add(rest[0][2], a_side, a_far), add(rest[1][2], b_far, b_side)], axis=1
    ).reshape(columns, rows, width)
    arrived = [
        shift(lax.dynamic_index_in_dim(total, (line + k) % columns, 0, keepdims=False), "line", k)
        for k in range(1, columns)
    ]
    return add(lax.dynamic_index_in_dim(total, line, 0, keepdims=False), *arrived)


def on_device(
    tokens,
    queries,
    suffix_keys,
    suffix_values,
    prefix_keys,
    prefix_values,
    out_weight,
    norm_gain,
    routes,
    route_weights,
    gate_up_weight,
    down_weight,
):
    rows_here, width = tokens.shape
    devices = lax.axis_size(ALL)
    experts = devices // 2
    capacity = 4 * rows_here * TOP // (3 * experts)
    gather_fits = devices * rows_here * width * 2 <= GATHER_BUDGET
    kv = jnp.concatenate([prefix_keys, prefix_values])
    weights = [gate_up_weight[0], down_weight[0]]
    if gather_fits:
        lines = [kv] + [shift(kv, "line", k) for k in range(1, lax.axis_size("line"))]
        pieces = lines + [swap(piece, "side") for piece in lines]
        weights = weights + [swap(one, "core") for one in weights]
        table = lax.all_gather(
            jnp.concatenate([routes.T.astype(jnp.float32), route_weights.T]),
            ("far", "line", "side"),
            axis=0,
        )
    else:
        pieces = [
            lax.all_gather(kv, ("line", "side"), axis=1, tiled=True)
        ]
    heads_out = attention(queries, suffix_keys, suffix_values, pieces)
    attended, normed = project(heads_out, out_weight, tokens, norm_gain)
    if gather_fits:
        routed = gather_plan(normed, table, weights, capacity)
    else:
        routed = exchange_plan(
            normed, routes, route_weights, weights[0], weights[1], experts, capacity
        )
    return (attended, routed)


def solution(mesh):
    groups, members = mesh.shape["grp"], mesh.shape["dev"]
    fine = Mesh(mesh.devices.reshape(groups // 2, 2, members // 2, 2), ALL)
    rows = P(ALL, None)
    prefix = P(("far", "core"), ("line", "side"), None)
    stacked = P(ALL, None, None)
    return jax.shard_map(
        on_device,
        mesh=fine,
        in_specs=(rows,) * 4
        + (prefix, prefix, P(), P(), rows, rows, stacked, stacked),
        out_specs=(rows, rows),
        check_vma=False,
    )
```

```python
import math

import jax
import jax.numpy as jnp
from jax import lax
from jax.experimental import pallas as pl
from jax.experimental.pallas import tpu as pltpu
from jax.sharding import Mesh
from jax.sharding import PartitionSpec as P

HEADS = 16
HEAD_DIM = 128
TOP = 6
ALL = ("far", "core", "line", "side")
GATHER_BUDGET = 40 * 2**20
VMEM_LIMIT = 52 * 2**20
EXPERT_VMEM = 36 * 2**20


def attention_kernel(q_ref, sk_ref, sv_ref, *refs):
    pieces, out_ref = refs[:-1], refs[-1]
    rows = q_ref.shape[0]
    span = q_ref.shape[1]
    scale = 1.0 / math.sqrt(HEAD_DIM)
    causal = lax.broadcasted_iota(jnp.int32, (rows, rows), 0) >= lax.broadcasted_iota(
        jnp.int32, (rows, rows), 1
    )
    contract = (((1,), (1,)), ((), ()))
    for head in range(span // HEAD_DIM):
        cols = slice(head * HEAD_DIM, (head + 1) * HEAD_DIM)
        query = q_ref[:, cols]
        keys = jnp.concatenate([piece[0, :, cols] for piece in pieces])
        values = jnp.concatenate([piece[1, :, cols] for piece in pieces])
        prefix = (
            lax.dot_general(query, keys, contract, preferred_element_type=jnp.float32) * scale
        )
        suffix = (
            lax.dot_general(query, sk_ref[:, cols], contract, preferred_element_type=jnp.float32)
            * scale
        )
        suffix = jnp.where(causal, suffix, -jnp.inf)
        top = jnp.maximum(
            jnp.max(prefix, axis=1, keepdims=True), jnp.max(suffix, axis=1, keepdims=True)
        )
        prefix = jnp.exp(prefix - top)
        suffix = jnp.exp(suffix - top)
        total = jnp.sum(prefix, axis=1, keepdims=True) + jnp.sum(suffix, axis=1, keepdims=True)
        mixed = jnp.dot(
            prefix.astype(jnp.bfloat16), values, preferred_element_type=jnp.float32
        ) + jnp.dot(
            suffix.astype(jnp.bfloat16), sv_ref[:, cols], preferred_element_type=jnp.float32
        )
        out_ref[:, cols] = (mixed / total).astype(jnp.bfloat16)


def attention(queries, suffix_keys, suffix_values, pieces):
    rows, width = queries.shape
    span = 4 * HEAD_DIM
    by_cols = pl.BlockSpec((rows, span), lambda i: (0, i))
    return pl.pallas_call(
        attention_kernel,
        grid=(width // span,),
        in_specs=[by_cols] * 3
        + [pl.BlockSpec(piece.shape[:2] + (span,), lambda i: (0, 0, i)) for piece in pieces],
        out_specs=by_cols,
        out_shape=jax.ShapeDtypeStruct((rows, width), jnp.bfloat16),
        compiler_params=pltpu.CompilerParams(vmem_limit_bytes=VMEM_LIMIT),
        name="attention",
    )(queries, suffix_keys, suffix_values, *pieces)


def project_kernel(heads_ref, weight_ref, tokens_ref, gain_ref, attended_ref, normed_ref, held):
    step = pl.program_id(0)
    attended = jnp.dot(
        heads_ref[...], weight_ref[...], preferred_element_type=jnp.float32
    ).astype(jnp.bfloat16)
    attended_ref[...] = attended
    held[step] = tokens_ref[...].astype(jnp.float32) + attended.astype(jnp.float32)

    @pl.when(step == pl.num_programs(0) - 1)
    def finish():
        steps, rows, span = held.shape
        squares = jnp.zeros((rows, 1), jnp.float32)
        for piece in range(steps):
            part = held[piece]
            squares = squares + jnp.sum(part * part, axis=1, keepdims=True)
        factor = lax.rsqrt(squares / (steps * span) + 1e-06)
        for piece in range(steps):
            cols = slice(piece * span, (piece + 1) * span)
            normed_ref[:, cols] = (held[piece] * factor * gain_ref[:, cols]).astype(jnp.bfloat16)


def project(heads_out, out_weight, tokens, norm_gain):
    rows, width = tokens.shape
    span = 512
    steps = width // span
    by_cols = pl.BlockSpec((rows, span), lambda i: (0, i))
    return pl.pallas_call(
        project_kernel,
        grid=(steps,),
        in_specs=[
            pl.BlockSpec((rows, width), lambda i: (0, 0)),
            pl.BlockSpec((width, span), lambda i: (0, i)),
            by_cols,
            pl.BlockSpec((1, width), lambda i: (0, 0)),
        ],
        out_specs=[by_cols, pl.BlockSpec((rows, width), lambda i: (0, 0))],
        out_shape=[
            jax.ShapeDtypeStruct((rows, width), jnp.bfloat16),
            jax.ShapeDtypeStruct((rows, width), jnp.bfloat16),
        ],
        scratch_shapes=[pltpu.VMEM((steps, rows, span), jnp.float32)],
        compiler_params=pltpu.CompilerParams(vmem_limit_bytes=VMEM_LIMIT),
        name="project_and_norm",
    )(heads_out, out_weight, tokens, norm_gain.reshape(1, width))


def experts_kernel(capacity, count, slot_ref, gate_ref, *refs):
    rows_refs, refs = refs[:count], refs[count:]
    weight_refs, refs = refs[:4], refs[4:]
    out_refs, refs = refs[:count], refs[count:]
    picked, scaled, held, arrived = refs[0], refs[1], refs[2:6], refs[6]
    copies = [
        pltpu.make_async_copy(source, target, arrived.at[i])
        for i, (source, target) in enumerate(zip(weight_refs, held))
    ]
    for copy in copies:
        copy.start()
    rows = rows_refs[0].shape[0]
    hidden = held[1].shape[0]
    levels = lax.broadcasted_iota(jnp.int32, (2 * capacity, rows), 0)
    for one in range(count):
        chosen = (levels == slot_ref[one, 0]) | (levels == slot_ref[one, 1])
        taken = jnp.dot(
            chosen.astype(jnp.bfloat16), rows_refs[one][...], preferred_element_type=jnp.float32
        ).astype(jnp.bfloat16)
        picked[0, one * capacity : (one + 1) * capacity, :] = taken[:capacity]
        picked[1, one * capacity : (one + 1) * capacity, :] = taken[capacity:]
    for which in range(2):
        low = which * capacity
        copies[2 * which].wait()
        projected = jnp.dot(
            picked[which], held[2 * which][...], preferred_element_type=jnp.float32
        )
        gate = projected[:, :hidden]
        active = (gate / (1.0 + jnp.exp(-gate)) * projected[:, hidden:]).astype(jnp.bfloat16)
        copies[2 * which + 1].wait()
        result = jnp.dot(active, held[2 * which + 1][...], preferred_element_type=jnp.float32)
        for one in range(count):
            chosen = levels[low : low + capacity] == slot_ref[one, which]
            gates = jnp.sum(
                jnp.where(chosen, gate_ref[one, which], 0.0), axis=1, keepdims=True
            )
            scaled[one, low : low + capacity, :] = (
                result[one * capacity : (one + 1) * capacity, :] * gates
            ).astype(jnp.bfloat16)
    for one in range(count):
        chosen = (levels == slot_ref[one, 0]) | (levels == slot_ref[one, 1])
        out_refs[one][...] = lax.dot_general(
            chosen.astype(jnp.bfloat16),
            scaled[one],
            (((0,), (0,)), ((), ())),
            preferred_element_type=jnp.float32,
        ).astype(jnp.bfloat16)


def run_experts(blocks, slots, gates, weights, capacity):
    count = len(blocks)
    rows, width = blocks[0].shape
    hidden = weights[1].shape[0]
    total = 2 * count * capacity
    local = pl.BlockSpec(memory_space=pltpu.VMEM)
    return pl.pallas_call(
        lambda *refs: experts_kernel(capacity, count, *refs),
        in_specs=[local] * (2 + count) + [pl.BlockSpec(memory_space=pl.ANY)] * 4,
        out_specs=[local] * count,
        out_shape=[jax.ShapeDtypeStruct((rows, width), jnp.bfloat16)] * count,
        scratch_shapes=[
            pltpu.VMEM((2, count * capacity, width), jnp.bfloat16),
            pltpu.VMEM((count, 2 * capacity, width), jnp.bfloat16),
        ]
        + [pltpu.VMEM(one.shape, jnp.bfloat16) for one in weights]
        + [pltpu.SemaphoreType.DMA((4,))],
        compiler_params=pltpu.CompilerParams(vmem_limit_bytes=EXPERT_VMEM),
        cost_estimate=pl.CostEstimate(
            flops=total * width * hidden * 6,
            bytes_accessed=sum(one.size * 2 for one in weights) + count * rows * width * 4,
            transcendentals=total * hidden,
        ),
        name="experts",
    )(slots, gates, *blocks, *weights)


def half_expert(rows, gate_up, down_proj):
    hidden_units = down_proj.shape[0]
    projected = jnp.dot(rows, gate_up, preferred_element_type=jnp.float32)
    active = (jax.nn.silu(projected[:, :hidden_units]) * projected[:, hidden_units:]).astype(
        jnp.bfloat16
    )
    return jnp.dot(active, down_proj, preferred_element_type=jnp.float32).astype(jnp.bfloat16)


def exchange_plan(normed, routes, route_weights, gate_up, down, experts, capacity):
    rows_here, width = normed.shape
    flat_routes = routes.reshape(-1)
    onehot = (flat_routes[:, None] == jnp.arange(experts, dtype=jnp.int32)[None, :]).astype(
        jnp.int32
    )
    ranking = jnp.sum(jnp.cumsum(onehot, axis=0) * onehot, axis=1) - 1
    slots = flat_routes * capacity + ranking
    owners = jnp.arange(rows_here * TOP, dtype=jnp.int32) // TOP
    outgoing = jnp.zeros((experts * capacity, width), jnp.bfloat16).at[slots].set(normed[owners])
    buffer = jnp.broadcast_to(
        outgoing.reshape(experts, 1, capacity, width), (experts, 2, capacity, width)
    ).reshape(2 * experts, capacity, width)
    received = lax.all_to_all(buffer, ALL, split_axis=0, concat_axis=0, tiled=True)
    partial_rows = half_expert(received.reshape(-1, width), gate_up, down).reshape(
        2 * experts, capacity, width
    )
    returned = lax.all_to_all(partial_rows, ALL, split_axis=0, concat_axis=0, tiled=True)
    halves = returned.reshape(experts, 2, capacity, width)
    expert_table = lax.optimization_barrier(
        (halves[:, 0].astype(jnp.float32) + halves[:, 1].astype(jnp.float32)).astype(jnp.bfloat16)
    ).reshape(experts * capacity, width)
    picked = expert_table[slots].astype(jnp.float32)
    weighted_rows = picked * route_weights.reshape(-1)[:, None]
    return jnp.sum(weighted_rows.reshape(rows_here, TOP, width), axis=1).astype(jnp.bfloat16)


def own_slots(table, mine, first_slot):
    named = table[:, :TOP] == mine.astype(jnp.float32)
    gates = jnp.sum(jnp.where(named, table[:, TOP:], 0.0), axis=1)
    member = jnp.any(named, axis=1)
    rows = table.shape[-1]
    before = jnp.arange(rows)[:, None] <= jnp.arange(rows)[None, :]
    ranks = jnp.dot(
        member.astype(jnp.bfloat16),
        before.astype(jnp.bfloat16),
        preferred_element_type=jnp.float32,
    ).astype(jnp.int32)
    return jnp.where(member, ranks - 1 + first_slot, -1), gates


def swap(array, axis):
    return lax.ppermute(array, axis, [(0, 1), (1, 0)])


def shift(array, axis, amount):
    size = lax.axis_size(axis)
    return lax.ppermute(array, axis, [(i, (i + amount) % size) for i in range(size)])


def add(*arrays):
    return sum(one.astype(jnp.float32) for one in arrays).astype(jnp.bfloat16)


def relative_slots(table, capacity):
    columns = lax.axis_size("line")
    far, core = lax.axis_index("far"), lax.axis_index("core")
    line, side = lax.axis_index("line"), lax.axis_index("side")
    places = jnp.arange(4 * columns)
    back, across, beside = places // 4, places // 2 % 2, places % 2
    source = ((far ^ across) * columns + (line - back + columns) % columns) * 2 + (side ^ beside)
    table = table[source]
    own = (far * 2 + core) * columns + line
    other = (far * 2 + 1 - core) * columns + line
    own_slot, own_gate = own_slots(table, own, 0)
    other_slot, other_gate = own_slots(table, other, capacity)
    shape = (columns, 4, 2, 1, -1)
    slots = jnp.stack([own_slot, other_slot], axis=1).reshape(shape)
    gates = jnp.stack([own_gate, other_gate], axis=1).reshape(shape)
    return slots, gates


def gather_plan(normed, slots, gates, weights, capacity):
    columns = lax.axis_size("line")
    arrived = []
    for back in range(columns):
        block = shift(normed, "line", back) if back else normed
        if back % 2 == 0:
            beside = swap(block, "side")
            across = swap(block, "far")
            corner = swap(beside, "far")
        else:
            across = swap(block, "far")
            beside = swap(block, "side")
            corner = swap(across, "side")
        results = run_experts(
            [block, beside, across, corner], slots[back], gates[back], weights, capacity
        )
        here, beside, across, corner = results
        if back % 2 == 0:
            across = add(across, swap(corner, "side"))
            total = add(here, swap(beside, "side"), swap(across, "far"))
        else:
            beside = add(beside, swap(corner, "far"))
            total = add(here, swap(across, "far"), swap(beside, "side"))
        arrived.append(shift(total, "line", -back) if back else total)
    return add(*arrived)


def on_device(
    tokens,
    queries,
    suffix_keys,
    suffix_values,
    prefix_keys,
    prefix_values,
    out_weight,
    norm_gain,
    routes,
    route_weights,
    gate_up_weight,
    down_weight,
):
    rows_here, width = tokens.shape
    devices = lax.axis_size(ALL)
    experts = devices // 2
    capacity = 4 * rows_here * TOP // (3 * experts)
    gather_fits = devices * rows_here * width * 2 <= GATHER_BUDGET
    kv = jnp.concatenate([prefix_keys, prefix_values])
    weights = [gate_up_weight[0], down_weight[0]]
    if gather_fits:
        lines = [kv] + [shift(kv, "line", k) for k in range(1, lax.axis_size("line"))]
        pieces = lines + [swap(piece, "side") for piece in lines]
        weights = weights + [swap(one, "core") for one in weights]
        table = lax.all_gather(
            jnp.concatenate([routes.T.astype(jnp.float32), route_weights.T]),
            ("far", "line", "side"),
            axis=0,
        )
        slots, gates = relative_slots(table, capacity)
        queries, slots, gates = lax.optimization_barrier((queries, slots, gates))
    else:
        pieces = [
            lax.all_gather(kv, ("line", "side"), axis=1, tiled=True)
        ]
    heads_out = attention(queries, suffix_keys, suffix_values, pieces)
    attended, normed = project(heads_out, out_weight, tokens, norm_gain)
    if gather_fits:
        routed = gather_plan(normed, slots, gates, weights, capacity)
    else:
        routed = exchange_plan(
            normed, routes, route_weights, weights[0], weights[1], experts, capacity
        )
    return (attended, routed)


def solution(mesh):
    groups, members = mesh.shape["grp"], mesh.shape["dev"]
    fine = Mesh(mesh.devices.reshape(groups // 2, 2, members // 2, 2), ALL)
    rows = P(ALL, None)
    prefix = P(("far", "core"), ("line", "side"), None)
    stacked = P(ALL, None, None)
    return jax.shard_map(
        on_device,
        mesh=fine,
        in_specs=(rows,) * 4
        + (prefix, prefix, P(), P(), rows, rows, stacked, stacked),
        out_specs=(rows, rows),
        check_vma=False,
    )
```

```python
import math

import jax
import jax.numpy as jnp
from jax import lax
from jax.experimental import pallas as pl
from jax.experimental.pallas import tpu as pltpu
from jax.sharding import Mesh
from jax.sharding import PartitionSpec as P

HEADS = 16
HEAD_DIM = 128
TOP = 6
ALL = ("far", "core", "line", "side")
GATHER_BUDGET = 40 * 2**20
VMEM_LIMIT = 52 * 2**20
EXPERT_VMEM = 36 * 2**20


def attention_kernel(q_ref, sk_ref, sv_ref, *refs):
    pieces, out_ref = refs[:-1], refs[-1]
    rows = q_ref.shape[0]
    span = q_ref.shape[1]
    scale = 1.0 / math.sqrt(HEAD_DIM)
    causal = lax.broadcasted_iota(jnp.int32, (rows, rows), 0) >= lax.broadcasted_iota(
        jnp.int32, (rows, rows), 1
    )
    contract = (((1,), (1,)), ((), ()))
    for head in range(span // HEAD_DIM):
        cols = slice(head * HEAD_DIM, (head + 1) * HEAD_DIM)
        query = q_ref[:, cols]
        keys = jnp.concatenate([piece[0, :, cols] for piece in pieces])
        values = jnp.concatenate([piece[1, :, cols] for piece in pieces])
        prefix = (
            lax.dot_general(query, keys, contract, preferred_element_type=jnp.float32) * scale
        )
        suffix = (
            lax.dot_general(query, sk_ref[:, cols], contract, preferred_element_type=jnp.float32)
            * scale
        )
        suffix = jnp.where(causal, suffix, -jnp.inf)
        top = jnp.maximum(
            jnp.max(prefix, axis=1, keepdims=True), jnp.max(suffix, axis=1, keepdims=True)
        )
        prefix = jnp.exp(prefix - top)
        suffix = jnp.exp(suffix - top)
        total = jnp.sum(prefix, axis=1, keepdims=True) + jnp.sum(suffix, axis=1, keepdims=True)
        mixed = jnp.dot(
            prefix.astype(jnp.bfloat16), values, preferred_element_type=jnp.float32
        ) + jnp.dot(
            suffix.astype(jnp.bfloat16), sv_ref[:, cols], preferred_element_type=jnp.float32
        )
        out_ref[:, cols] = (mixed / total).astype(jnp.bfloat16)


def attention(queries, suffix_keys, suffix_values, pieces):
    rows, width = queries.shape
    span = 4 * HEAD_DIM
    by_cols = pl.BlockSpec((rows, span), lambda i: (0, i))
    return pl.pallas_call(
        attention_kernel,
        grid=(width // span,),
        in_specs=[by_cols] * 3
        + [pl.BlockSpec(piece.shape[:2] + (span,), lambda i: (0, 0, i)) for piece in pieces],
        out_specs=by_cols,
        out_shape=jax.ShapeDtypeStruct((rows, width), jnp.bfloat16),
        compiler_params=pltpu.CompilerParams(vmem_limit_bytes=VMEM_LIMIT),
        name="attention",
    )(queries, suffix_keys, suffix_values, *pieces)


def project_kernel(heads_ref, weight_ref, tokens_ref, gain_ref, attended_ref, normed_ref, held):
    step = pl.program_id(0)
    attended = jnp.dot(
        heads_ref[...], weight_ref[...], preferred_element_type=jnp.float32
    ).astype(jnp.bfloat16)
    attended_ref[...] = attended
    held[step] = tokens_ref[...].astype(jnp.float32) + attended.astype(jnp.float32)

    @pl.when(step == pl.num_programs(0) - 1)
    def finish():
        steps, rows, span = held.shape
        squares = jnp.zeros((rows, 1), jnp.float32)
        for piece in range(steps):
            part = held[piece]
            squares = squares + jnp.sum(part * part, axis=1, keepdims=True)
        factor = lax.rsqrt(squares / (steps * span) + 1e-06)
        for piece in range(steps):
            cols = slice(piece * span, (piece + 1) * span)
            normed_ref[:, cols] = (held[piece] * factor * gain_ref[:, cols]).astype(jnp.bfloat16)


def project(heads_out, out_weight, tokens, norm_gain):
    rows, width = tokens.shape
    span = 512
    steps = width // span
    by_cols = pl.BlockSpec((rows, span), lambda i: (0, i))
    return pl.pallas_call(
        project_kernel,
        grid=(steps,),
        in_specs=[
            pl.BlockSpec((rows, width), lambda i: (0, 0)),
            pl.BlockSpec((width, span), lambda i: (0, i)),
            by_cols,
            pl.BlockSpec((1, width), lambda i: (0, 0)),
        ],
        out_specs=[by_cols, pl.BlockSpec((rows, width), lambda i: (0, 0))],
        out_shape=[
            jax.ShapeDtypeStruct((rows, width), jnp.bfloat16),
            jax.ShapeDtypeStruct((rows, width), jnp.bfloat16),
        ],
        scratch_shapes=[pltpu.VMEM((steps, rows, span), jnp.float32)],
        compiler_params=pltpu.CompilerParams(vmem_limit_bytes=VMEM_LIMIT),
        name="project_and_norm",
    )(heads_out, out_weight, tokens, norm_gain.reshape(1, width))


def experts_kernel(capacity, count, slot_ref, gate_ref, *refs):
    rows_refs, refs = refs[:count], refs[count:]
    weight_refs, refs = refs[:4], refs[4:]
    out_refs, refs = refs[:count], refs[count:]
    picked, scaled, held, arrived = refs[0], refs[1], refs[2:6], refs[6]
    copies = [
        pltpu.make_async_copy(source, target, arrived.at[i])
        for i, (source, target) in enumerate(zip(weight_refs, held))
    ]
    for copy in copies:
        copy.start()
    rows = rows_refs[0].shape[0]
    hidden = held[1].shape[0]
    levels = lax.broadcasted_iota(jnp.int32, (2 * capacity, rows), 0)
    for one in range(count):
        chosen = (levels == slot_ref[one, 0]) | (levels == slot_ref[one, 1])
        taken = jnp.dot(
            chosen.astype(jnp.bfloat16), rows_refs[one][...], preferred_element_type=jnp.float32
        ).astype(jnp.bfloat16)
        picked[0, one * capacity : (one + 1) * capacity, :] = taken[:capacity]
        picked[1, one * capacity : (one + 1) * capacity, :] = taken[capacity:]
    for which in range(2):
        low = which * capacity
        copies[2 * which].wait()
        projected = jnp.dot(
            picked[which], held[2 * which][...], preferred_element_type=jnp.float32
        )
        gate = projected[:, :hidden]
        active = (gate / (1.0 + jnp.exp(-gate)) * projected[:, hidden:]).astype(jnp.bfloat16)
        copies[2 * which + 1].wait()
        result = jnp.dot(active, held[2 * which + 1][...], preferred_element_type=jnp.float32)
        for one in range(count):
            chosen = levels[low : low + capacity] == slot_ref[one, which]
            gates = jnp.sum(
                jnp.where(chosen, gate_ref[one, which], 0.0), axis=1, keepdims=True
            )
            scaled[one, low : low + capacity, :] = (
                result[one * capacity : (one + 1) * capacity, :] * gates
            ).astype(jnp.bfloat16)
    for one in range(count):
        chosen = (levels == slot_ref[one, 0]) | (levels == slot_ref[one, 1])
        out_refs[one][...] = lax.dot_general(
            chosen.astype(jnp.bfloat16),
            scaled[one],
            (((0,), (0,)), ((), ())),
            preferred_element_type=jnp.float32,
        ).astype(jnp.bfloat16)


def run_experts(blocks, slots, gates, weights, capacity):
    count = len(blocks)
    rows, width = blocks[0].shape
    hidden = weights[1].shape[0]
    total = 2 * count * capacity
    local = pl.BlockSpec(memory_space=pltpu.VMEM)
    return pl.pallas_call(
        lambda *refs: experts_kernel(capacity, count, *refs),
        in_specs=[local] * (2 + count) + [pl.BlockSpec(memory_space=pl.ANY)] * 4,
        out_specs=[local] * count,
        out_shape=[jax.ShapeDtypeStruct((rows, width), jnp.bfloat16)] * count,
        scratch_shapes=[
            pltpu.VMEM((2, count * capacity, width), jnp.bfloat16),
            pltpu.VMEM((count, 2 * capacity, width), jnp.bfloat16),
        ]
        + [pltpu.VMEM(one.shape, jnp.bfloat16) for one in weights]
        + [pltpu.SemaphoreType.DMA((4,))],
        compiler_params=pltpu.CompilerParams(vmem_limit_bytes=EXPERT_VMEM),
        cost_estimate=pl.CostEstimate(
            flops=total * width * hidden * 6,
            bytes_accessed=sum(one.size * 2 for one in weights) + count * rows * width * 4,
            transcendentals=total * hidden,
        ),
        name="experts",
    )(slots, gates, *blocks, *weights)


def half_expert(rows, gate_up, down_proj):
    hidden_units = down_proj.shape[0]
    projected = jnp.dot(rows, gate_up, preferred_element_type=jnp.float32)
    active = (jax.nn.silu(projected[:, :hidden_units]) * projected[:, hidden_units:]).astype(
        jnp.bfloat16
    )
    return jnp.dot(active, down_proj, preferred_element_type=jnp.float32).astype(jnp.bfloat16)


def exchange_plan(normed, routes, route_weights, gate_up, down, experts, capacity):
    rows_here, width = normed.shape
    flat_routes = routes.reshape(-1)
    onehot = (flat_routes[:, None] == jnp.arange(experts, dtype=jnp.int32)[None, :]).astype(
        jnp.int32
    )
    ranking = jnp.sum(jnp.cumsum(onehot, axis=0) * onehot, axis=1) - 1
    slots = flat_routes * capacity + ranking
    owners = jnp.arange(rows_here * TOP, dtype=jnp.int32) // TOP
    outgoing = jnp.zeros((experts * capacity, width), jnp.bfloat16).at[slots].set(normed[owners])
    buffer = jnp.broadcast_to(
        outgoing.reshape(experts, 1, capacity, width), (experts, 2, capacity, width)
    ).reshape(2 * experts, capacity, width)
    received = lax.all_to_all(buffer, ALL, split_axis=0, concat_axis=0, tiled=True)
    partial_rows = half_expert(received.reshape(-1, width), gate_up, down).reshape(
        2 * experts, capacity, width
    )
    returned = lax.all_to_all(partial_rows, ALL, split_axis=0, concat_axis=0, tiled=True)
    halves = returned.reshape(experts, 2, capacity, width)
    expert_table = lax.optimization_barrier(
        (halves[:, 0].astype(jnp.float32) + halves[:, 1].astype(jnp.float32)).astype(jnp.bfloat16)
    ).reshape(experts * capacity, width)
    picked = expert_table[slots].astype(jnp.float32)
    weighted_rows = picked * route_weights.reshape(-1)[:, None]
    return jnp.sum(weighted_rows.reshape(rows_here, TOP, width), axis=1).astype(jnp.bfloat16)


def own_slots(table, mine, first_slot):
    named = table[:, :TOP] == mine.astype(jnp.float32)
    gates = jnp.sum(jnp.where(named, table[:, TOP:], 0.0), axis=1)
    member = jnp.any(named, axis=1)
    rows = table.shape[-1]
    before = jnp.arange(rows)[:, None] <= jnp.arange(rows)[None, :]
    ranks = jnp.dot(
        member.astype(jnp.bfloat16),
        before.astype(jnp.bfloat16),
        preferred_element_type=jnp.float32,
    ).astype(jnp.int32)
    return jnp.where(member, ranks - 1 + first_slot, -1), gates


def swap(array, axis):
    return lax.ppermute(array, axis, [(0, 1), (1, 0)])


def shift(array, axis, amount):
    size = lax.axis_size(axis)
    return lax.ppermute(array, axis, [(i, (i + amount) % size) for i in range(size)])


def add(*arrays):
    return sum(one.astype(jnp.float32) for one in arrays).astype(jnp.bfloat16)


def relative_slots(routes, route_weights, capacity):
    columns = lax.axis_size("line")
    far, core, line = lax.axis_index("far"), lax.axis_index("core"), lax.axis_index("line")
    table = jnp.concatenate([routes.T.astype(jnp.float32), route_weights.T])
    table = jnp.stack([table] + [shift(table, "line", back) for back in range(1, columns)])
    table = jnp.stack([table, swap(table, "side")])
    table = jnp.stack([table, swap(table, "far")])
    table = table.reshape((4 * columns,) + table.shape[3:])
    own = (far * 2 + core) * columns + line
    other = (far * 2 + 1 - core) * columns + line
    own_slot, own_gate = own_slots(table, own, 0)
    other_slot, other_gate = own_slots(table, other, capacity)
    shape = (4, columns, 2, 1, -1)
    slots = jnp.stack([own_slot, other_slot], axis=1).reshape(shape)
    gates = jnp.stack([own_gate, other_gate], axis=1).reshape(shape)
    return slots, gates


def go_home(results, back):
    here, beside, across, corner = results
    if back % 2 == 0:
        across = add(across, swap(corner, "side"))
        total = add(here, swap(beside, "side"), swap(across, "far"))
    else:
        beside = add(beside, swap(corner, "far"))
        total = add(here, swap(across, "far"), swap(beside, "side"))
    return shift(total, "line", -back) if back else total


def gather_plan(normed, slots, gates, weights, capacity):
    columns = lax.axis_size("line")
    normed, weights = lax.optimization_barrier((normed, weights))
    results = []
    for back in range(columns):
        block = shift(normed, "line", back) if back else normed
        if back % 2 == 0:
            beside = swap(block, "side")
            across = swap(block, "far")
            corner = swap(beside, "far")
        else:
            across = swap(block, "far")
            beside = swap(block, "side")
            corner = swap(across, "side")
        mine = slots[:, back]
        if back:
            mine, results[-1][0] = lax.optimization_barrier((mine, results[-1][0]))
        results.append(
            list(
                run_experts(
                    [block, beside, across, corner], mine, gates[:, back], weights, capacity
                )
            )
        )
    results[0], results[-1] = lax.optimization_barrier((results[0], results[-1]))
    return add(*[go_home(results[back], back) for back in range(columns)])


def on_device(
    tokens,
    queries,
    suffix_keys,
    suffix_values,
    prefix_keys,
    prefix_values,
    out_weight,
    norm_gain,
    routes,
    route_weights,
    gate_up_weight,
    down_weight,
):
    rows_here, width = tokens.shape
    devices = lax.axis_size(ALL)
    experts = devices // 2
    capacity = 4 * rows_here * TOP // (3 * experts)
    gather_fits = devices * rows_here * width * 2 <= GATHER_BUDGET
    kv = jnp.concatenate([prefix_keys, prefix_values])
    weights = [gate_up_weight[0], down_weight[0]]
    if gather_fits:
        lines = [kv] + [shift(kv, "line", k) for k in range(1, lax.axis_size("line"))]
        pieces = lines + [swap(piece, "side") for piece in lines]
        weights = weights + [swap(one, "core") for one in weights]
        slots, gates = relative_slots(routes, route_weights, capacity)
        queries, slots, gates = lax.optimization_barrier((queries, slots, gates))
    else:
        pieces = [
            lax.all_gather(kv, ("line", "side"), axis=1, tiled=True)
        ]
    heads_out = attention(queries, suffix_keys, suffix_values, pieces)
    attended, normed = project(heads_out, out_weight, tokens, norm_gain)
    if gather_fits:
        routed = gather_plan(normed, slots, gates, weights, capacity)
    else:
        routed = exchange_plan(
            normed, routes, route_weights, weights[0], weights[1], experts, capacity
        )
    return (attended, routed)


def solution(mesh):
    groups, members = mesh.shape["grp"], mesh.shape["dev"]
    fine = Mesh(mesh.devices.reshape(groups // 2, 2, members // 2, 2), ALL)
    rows = P(ALL, None)
    prefix = P(("far", "core"), ("line", "side"), None)
    stacked = P(ALL, None, None)
    return jax.shard_map(
        on_device,
        mesh=fine,
        in_specs=(rows,) * 4
        + (prefix, prefix, P(), P(), rows, rows, stacked, stacked),
        out_specs=(rows, rows),
        check_vma=False,
    )
```

```python
import math

import jax
import jax.numpy as jnp
from jax import lax
from jax.experimental import pallas as pl
from jax.experimental.pallas import tpu as pltpu
from jax.sharding import Mesh
from jax.sharding import PartitionSpec as P

HEADS = 16
HEAD_DIM = 128
TOP = 6
ALL = ("far", "core", "line", "side")
GATHER_BUDGET = 40 * 2**20
VMEM_LIMIT = 52 * 2**20
EXPERT_VMEM = 36 * 2**20


def attention_kernel(q_ref, sk_ref, sv_ref, *refs):
    pieces, out_ref = refs[:-1], refs[-1]
    rows = q_ref.shape[0]
    span = q_ref.shape[1]
    scale = 1.0 / math.sqrt(HEAD_DIM)
    causal = lax.broadcasted_iota(jnp.int32, (rows, rows), 0) >= lax.broadcasted_iota(
        jnp.int32, (rows, rows), 1
    )
    contract = (((1,), (1,)), ((), ()))
    for head in range(span // HEAD_DIM):
        cols = slice(head * HEAD_DIM, (head + 1) * HEAD_DIM)
        query = q_ref[:, cols]
        keys = jnp.concatenate([piece[0, :, cols] for piece in pieces])
        values = jnp.concatenate([piece[1, :, cols] for piece in pieces])
        prefix = (
            lax.dot_general(query, keys, contract, preferred_element_type=jnp.float32) * scale
        )
        suffix = (
            lax.dot_general(query, sk_ref[:, cols], contract, preferred_element_type=jnp.float32)
            * scale
        )
        suffix = jnp.where(causal, suffix, -jnp.inf)
        top = jnp.maximum(
            jnp.max(prefix, axis=1, keepdims=True), jnp.max(suffix, axis=1, keepdims=True)
        )
        prefix = jnp.exp(prefix - top)
        suffix = jnp.exp(suffix - top)
        total = jnp.sum(prefix, axis=1, keepdims=True) + jnp.sum(suffix, axis=1, keepdims=True)
        mixed = jnp.dot(
            prefix.astype(jnp.bfloat16), values, preferred_element_type=jnp.float32
        ) + jnp.dot(
            suffix.astype(jnp.bfloat16), sv_ref[:, cols], preferred_element_type=jnp.float32
        )
        out_ref[:, cols] = (mixed / total).astype(jnp.bfloat16)


def attention(queries, suffix_keys, suffix_values, pieces):
    rows, width = queries.shape
    span = 4 * HEAD_DIM
    by_cols = pl.BlockSpec((rows, span), lambda i: (0, i))
    return pl.pallas_call(
        attention_kernel,
        grid=(width // span,),
        in_specs=[by_cols] * 3
        + [pl.BlockSpec(piece.shape[:2] + (span,), lambda i: (0, 0, i)) for piece in pieces],
        out_specs=by_cols,
        out_shape=jax.ShapeDtypeStruct((rows, width), jnp.bfloat16),
        compiler_params=pltpu.CompilerParams(vmem_limit_bytes=VMEM_LIMIT),
        cost_estimate=pl.CostEstimate(
            flops=12 * rows * rows * width, bytes_accessed=12 * rows * width, transcendentals=0
        ),
        name="attention",
    )(queries, suffix_keys, suffix_values, *pieces)


def project_kernel(heads_ref, weight_ref, tokens_ref, gain_ref, attended_ref, normed_ref, held):
    step = pl.program_id(0)
    attended = jnp.dot(
        heads_ref[...], weight_ref[...], preferred_element_type=jnp.float32
    ).astype(jnp.bfloat16)
    attended_ref[...] = attended
    held[step] = tokens_ref[...].astype(jnp.float32) + attended.astype(jnp.float32)

    @pl.when(step == pl.num_programs(0) - 1)
    def finish():
        steps, rows, span = held.shape
        squares = jnp.zeros((rows, 1), jnp.float32)
        for piece in range(steps):
            part = held[piece]
            squares = squares + jnp.sum(part * part, axis=1, keepdims=True)
        factor = lax.rsqrt(squares / (steps * span) + 1e-06)
        for piece in range(steps):
            cols = slice(piece * span, (piece + 1) * span)
            normed_ref[:, cols] = (held[piece] * factor * gain_ref[:, cols]).astype(jnp.bfloat16)


def project(heads_out, out_weight, tokens, norm_gain):
    rows, width = tokens.shape
    span = 512
    steps = width // span
    by_cols = pl.BlockSpec((rows, span), lambda i: (0, i))
    return pl.pallas_call(
        project_kernel,
        grid=(steps,),
        in_specs=[
            pl.BlockSpec((rows, width), lambda i: (0, 0)),
            pl.BlockSpec((width, span), lambda i: (0, i)),
            by_cols,
            pl.BlockSpec((1, width), lambda i: (0, 0)),
        ],
        out_specs=[by_cols, pl.BlockSpec((rows, width), lambda i: (0, 0))],
        out_shape=[
            jax.ShapeDtypeStruct((rows, width), jnp.bfloat16),
            jax.ShapeDtypeStruct((rows, width), jnp.bfloat16),
        ],
        scratch_shapes=[pltpu.VMEM((steps, rows, span), jnp.float32)],
        compiler_params=pltpu.CompilerParams(vmem_limit_bytes=VMEM_LIMIT),
        cost_estimate=pl.CostEstimate(
            flops=2 * rows * width * width, bytes_accessed=2 * width * width, transcendentals=0
        ),
        name="project_and_norm",
    )(heads_out, out_weight, tokens, norm_gain.reshape(1, width))


def experts_kernel(capacity, count, slot_ref, gate_ref, *refs):
    rows_refs, refs = refs[:count], refs[count:]
    weight_refs, refs = refs[:4], refs[4:]
    out_refs, refs = refs[:count], refs[count:]
    picked, scaled, held, arrived = refs[0], refs[1], refs[2:6], refs[6]
    copies = [
        pltpu.make_async_copy(source, target, arrived.at[i])
        for i, (source, target) in enumerate(zip(weight_refs, held))
    ]
    for copy in copies:
        copy.start()
    rows = rows_refs[0].shape[0]
    hidden = held[1].shape[0]
    levels = lax.broadcasted_iota(jnp.int32, (2 * capacity, rows), 0)
    for one in range(count):
        chosen = (levels == slot_ref[one, 0]) | (levels == slot_ref[one, 1])
        taken = jnp.dot(
            chosen.astype(jnp.bfloat16), rows_refs[one][...], preferred_element_type=jnp.float32
        ).astype(jnp.bfloat16)
        picked[0, one * capacity : (one + 1) * capacity, :] = taken[:capacity]
        picked[1, one * capacity : (one + 1) * capacity, :] = taken[capacity:]
    for which in range(2):
        low = which * capacity
        copies[2 * which].wait()
        projected = jnp.dot(
            picked[which], held[2 * which][...], preferred_element_type=jnp.float32
        )
        gate = projected[:, :hidden]
        active = (gate / (1.0 + jnp.exp(-gate)) * projected[:, hidden:]).astype(jnp.bfloat16)
        copies[2 * which + 1].wait()
        result = jnp.dot(active, held[2 * which + 1][...], preferred_element_type=jnp.float32)
        for one in range(count):
            chosen = levels[low : low + capacity] == slot_ref[one, which]
            gates = jnp.sum(
                jnp.where(chosen, gate_ref[one, which], 0.0), axis=1, keepdims=True
            )
            scaled[one, low : low + capacity, :] = (
                result[one * capacity : (one + 1) * capacity, :] * gates
            ).astype(jnp.bfloat16)
    for one in range(count):
        chosen = (levels == slot_ref[one, 0]) | (levels == slot_ref[one, 1])
        out_refs[one][...] = lax.dot_general(
            chosen.astype(jnp.bfloat16),
            scaled[one],
            (((0,), (0,)), ((), ())),
            preferred_element_type=jnp.float32,
        ).astype(jnp.bfloat16)


def run_experts(blocks, slots, gates, weights, capacity):
    count = len(blocks)
    rows, width = blocks[0].shape
    hidden = weights[1].shape[0]
    total = 2 * count * capacity
    local = pl.BlockSpec(memory_space=pltpu.VMEM)
    return pl.pallas_call(
        lambda *refs: experts_kernel(capacity, count, *refs),
        in_specs=[local] * (2 + count) + [pl.BlockSpec(memory_space=pl.ANY)] * 4,
        out_specs=[local] * count,
        out_shape=[jax.ShapeDtypeStruct((rows, width), jnp.bfloat16)] * count,
        scratch_shapes=[
            pltpu.VMEM((2, count * capacity, width), jnp.bfloat16),
            pltpu.VMEM((count, 2 * capacity, width), jnp.bfloat16),
        ]
        + [pltpu.VMEM(one.shape, jnp.bfloat16) for one in weights]
        + [pltpu.SemaphoreType.DMA((4,))],
        compiler_params=pltpu.CompilerParams(vmem_limit_bytes=EXPERT_VMEM),
        cost_estimate=pl.CostEstimate(
            flops=total * width * hidden * 6,
            bytes_accessed=sum(one.size * 2 for one in weights) + count * rows * width * 4,
            transcendentals=total * hidden,
        ),
        name="experts",
    )(slots, gates, *blocks, *weights)


def half_expert(rows, gate_up, down_proj):
    hidden_units = down_proj.shape[0]
    projected = jnp.dot(rows, gate_up, preferred_element_type=jnp.float32)
    active = (jax.nn.silu(projected[:, :hidden_units]) * projected[:, hidden_units:]).astype(
        jnp.bfloat16
    )
    return jnp.dot(active, down_proj, preferred_element_type=jnp.float32).astype(jnp.bfloat16)


def exchange_plan(normed, routes, route_weights, gate_up, down, experts, capacity):
    rows_here, width = normed.shape
    flat_routes = routes.reshape(-1)
    onehot = (flat_routes[:, None] == jnp.arange(experts, dtype=jnp.int32)[None, :]).astype(
        jnp.int32
    )
    ranking = jnp.sum(jnp.cumsum(onehot, axis=0) * onehot, axis=1) - 1
    slots = flat_routes * capacity + ranking
    owners = jnp.arange(rows_here * TOP, dtype=jnp.int32) // TOP
    outgoing = jnp.zeros((experts * capacity, width), jnp.bfloat16).at[slots].set(normed[owners])
    buffer = jnp.broadcast_to(
        outgoing.reshape(experts, 1, capacity, width), (experts, 2, capacity, width)
    ).reshape(2 * experts, capacity, width)
    received = lax.all_to_all(buffer, ALL, split_axis=0, concat_axis=0, tiled=True)
    partial_rows = half_expert(received.reshape(-1, width), gate_up, down).reshape(
        2 * experts, capacity, width
    )
    returned = lax.all_to_all(partial_rows, ALL, split_axis=0, concat_axis=0, tiled=True)
    halves = returned.reshape(experts, 2, capacity, width)
    expert_table = lax.optimization_barrier(
        (halves[:, 0].astype(jnp.float32) + halves[:, 1].astype(jnp.float32)).astype(jnp.bfloat16)
    ).reshape(experts * capacity, width)
    picked = expert_table[slots].astype(jnp.float32)
    weighted_rows = picked * route_weights.reshape(-1)[:, None]
    return jnp.sum(weighted_rows.reshape(rows_here, TOP, width), axis=1).astype(jnp.bfloat16)


def own_slots(table, mine, first_slot):
    named = table[:, :TOP] == mine.astype(jnp.float32)
    gates = jnp.sum(jnp.where(named, table[:, TOP:], 0.0), axis=1)
    member = jnp.any(named, axis=1)
    rows = table.shape[-1]
    before = jnp.arange(rows)[:, None] <= jnp.arange(rows)[None, :]
    ranks = jnp.dot(
        member.astype(jnp.bfloat16),
        before.astype(jnp.bfloat16),
        preferred_element_type=jnp.float32,
    ).astype(jnp.int32)
    return jnp.where(member, ranks - 1 + first_slot, -1), gates


def swap(array, axis):
    return lax.ppermute(array, axis, [(0, 1), (1, 0)])


def shift(array, axis, amount):
    size = lax.axis_size(axis)
    return lax.ppermute(array, axis, [(i, (i + amount) % size) for i in range(size)])


def add(*arrays):
    return sum(one.astype(jnp.float32) for one in arrays).astype(jnp.bfloat16)


def along_line(block):
    columns = lax.axis_size("line")
    blocks = {0: block}
    for back in nearest_first()[1:]:
        if back <= columns // 2:
            blocks[back] = shift(blocks[back - 1], "line", 1)
        else:
            blocks[back] = shift(blocks[(back + 1) % columns], "line", -1)
    return [blocks[back] for back in range(columns)]


def nearest_first():
    columns = lax.axis_size("line")
    return sorted(range(columns), key=lambda back: (min(back, columns - back), back))


def prefix_pieces(kv, table, weights):
    order = nearest_first()
    held, swapped = {0: kv}, {}
    ready = [0]
    for i in range(1, len(order), 2):
        fresh = order[i : i + 2]
        for back in fresh:
            step = 1 if back <= len(order) // 2 else -1
            held[back] = shift(held[(back - step) % len(order)], "line", step)
        for back in ready:
            swapped[back] = swap(held[back], "side")
        moved, crossed, table, weights = lax.optimization_barrier(
            ([held[back] for back in fresh], [swapped[back] for back in ready], table, weights)
        )
        if i == 1:
            others = [swap(one, "core") for one in weights]
        held.update(zip(fresh, moved))
        swapped.update(zip(ready, crossed))
        ready = fresh
    for back in ready:
        swapped[back] = swap(held[back], "side")
    tables = [table] + [shift(table, "line", back) for back in range(1, len(order))]
    tables, crossed = lax.optimization_barrier((tables, [swapped[back] for back in ready]))
    swapped.update(zip(ready, crossed))
    return list(held.values()) + list(swapped.values()), jnp.stack(tables), others


def relative_slots(table, capacity):
    columns = lax.axis_size("line")
    far, core, line = lax.axis_index("far"), lax.axis_index("core"), lax.axis_index("line")
    table = table.reshape((4 * columns,) + table.shape[3:])
    own = (far * 2 + core) * columns + line
    other = (far * 2 + 1 - core) * columns + line
    own_slot, own_gate = own_slots(table, own, 0)
    other_slot, other_gate = own_slots(table, other, capacity)
    shape = (4, columns, 2, 1, -1)
    slots = jnp.stack([own_slot, other_slot], axis=1).reshape(shape)
    gates = jnp.stack([own_gate, other_gate], axis=1).reshape(shape)
    return slots, gates


def over_plane(block, axes):
    first = swap(block, axes[0])
    second = swap(block, axes[1])
    corner = swap(first, axes[1])
    if axes[0] == "side":
        return [block, first, second, corner]
    return [block, second, first, corner]


def first_sums(results, axes):
    here, beside, across, corner = results
    near, rest = (beside, across) if axes[0] == "side" else (across, beside)
    return here, rest, swap(corner, axes[0]), swap(near, axes[0])


def last_sums(here, rest, corner, near, axes, back):
    total = add(here, near, swap(add(rest, corner), axes[1]))
    return shift(total, "line", -back) if back else total


def gather_plan(normed, slots, gates, weights, capacity):
    order = nearest_first()
    blocks = along_line(normed)
    axes = [("side", "far") if i % 2 == 0 else ("far", "side") for i in range(len(order))]
    sums, previous, own = {}, None, None
    for i, back in enumerate(order):
        plane = over_plane(blocks[back], axes[i])
        mine = slots[:, back]
        if i >= 3:
            mine, sums[i - 2] = lax.optimization_barrier((mine, sums[i - 2]))
        if i > 0:
            mine, previous = lax.optimization_barrier((mine, previous))
            if i == 1:
                own = previous
            else:
                sums[i - 1] = first_sums(previous, axes[i - 1])
        previous = run_experts(plane, mine, gates[:, back], weights, capacity)
    last = len(order) - 1
    sums[last] = first_sums(previous, axes[last])
    own, sums[last] = lax.optimization_barrier((own, sums[last]))
    sums[0] = first_sums(own, axes[0])
    return add(*[last_sums(*sums[i], axes[i], back) for i, back in enumerate(order)])


def on_device(
    tokens,
    queries,
    suffix_keys,
    suffix_values,
    prefix_keys,
    prefix_values,
    out_weight,
    norm_gain,
    routes,
    route_weights,
    gate_up_weight,
    down_weight,
):
    rows_here, width = tokens.shape
    devices = lax.axis_size(ALL)
    experts = devices // 2
    capacity = 4 * rows_here * TOP // (3 * experts)
    gather_fits = devices * rows_here * width * 2 <= GATHER_BUDGET
    kv = jnp.concatenate([prefix_keys, prefix_values])
    weights = [gate_up_weight[0], down_weight[0]]
    if gather_fits:
        table = jnp.concatenate([routes.T.astype(jnp.float32), route_weights.T])
        pieces, table, others = prefix_pieces(kv, table, weights)
        beside = swap(table, "side")
    else:
        pieces = [lax.all_gather(kv, ("line", "side"), axis=1, tiled=True)]
    heads_out = attention(queries, suffix_keys, suffix_values, pieces)
    if gather_fits:
        heads_out, beside = lax.optimization_barrier((heads_out, beside))
        table = jnp.stack([table, beside])
        across = swap(table, "far")
    attended, normed = project(heads_out, out_weight, tokens, norm_gain)
    if gather_fits:
        normed, others, across = lax.optimization_barrier((normed, others, across))
        slots, gates = relative_slots(jnp.stack([table, across]), capacity)
        routed = gather_plan(normed, slots, gates, weights + others, capacity)
    else:
        routed = exchange_plan(
            normed, routes, route_weights, weights[0], weights[1], experts, capacity
        )
    return (attended, routed)


def solution(mesh):
    groups, members = mesh.shape["grp"], mesh.shape["dev"]
    fine = Mesh(mesh.devices.reshape(groups // 2, 2, members // 2, 2), ALL)
    rows = P(ALL, None)
    prefix = P(("far", "core"), ("line", "side"), None)
    stacked = P(ALL, None, None)
    return jax.shard_map(
        on_device,
        mesh=fine,
        in_specs=(rows,) * 4
        + (prefix, prefix, P(), P(), rows, rows, stacked, stacked),
        out_specs=(rows, rows),
        check_vma=False,
    )
```

```python
import math

import jax
import jax.numpy as jnp
from jax import lax
from jax.experimental import pallas as pl
from jax.experimental.pallas import tpu as pltpu
from jax.sharding import Mesh
from jax.sharding import PartitionSpec as P

HEADS = 16
HEAD_DIM = 128
TOP = 6
ALL = ("far", "core", "line", "side")
GATHER_BUDGET = 40 * 2**20
VMEM_LIMIT = 20 * 2**20
EXPERT_VMEM = 32 * 2**20


def attention_kernel(q_ref, sk_ref, sv_ref, *refs):
    pieces, out_ref = refs[:-1], refs[-1]
    rows = q_ref.shape[0]
    span = q_ref.shape[1]
    scale = 1.0 / math.sqrt(HEAD_DIM)
    causal = lax.broadcasted_iota(jnp.int32, (rows, rows), 0) >= lax.broadcasted_iota(
        jnp.int32, (rows, rows), 1
    )
    contract = (((1,), (1,)), ((), ()))
    for head in range(span // HEAD_DIM):
        cols = slice(head * HEAD_DIM, (head + 1) * HEAD_DIM)
        query = q_ref[:, cols]
        keys = jnp.concatenate([piece[0, :, cols] for piece in pieces])
        values = jnp.concatenate([piece[1, :, cols] for piece in pieces])
        prefix = (
            lax.dot_general(query, keys, contract, preferred_element_type=jnp.float32) * scale
        )
        suffix = (
            lax.dot_general(query, sk_ref[:, cols], contract, preferred_element_type=jnp.float32)
            * scale
        )
        suffix = jnp.where(causal, suffix, -jnp.inf)
        top = jnp.maximum(
            jnp.max(prefix, axis=1, keepdims=True), jnp.max(suffix, axis=1, keepdims=True)
        )
        prefix = jnp.exp(prefix - top)
        suffix = jnp.exp(suffix - top)
        total = jnp.sum(prefix, axis=1, keepdims=True) + jnp.sum(suffix, axis=1, keepdims=True)
        mixed = jnp.dot(
            prefix.astype(jnp.bfloat16), values, preferred_element_type=jnp.float32
        ) + jnp.dot(
            suffix.astype(jnp.bfloat16), sv_ref[:, cols], preferred_element_type=jnp.float32
        )
        out_ref[:, cols] = (mixed / total).astype(jnp.bfloat16)


def attention(queries, suffix_keys, suffix_values, pieces):
    rows, width = queries.shape
    span = 4 * HEAD_DIM
    by_cols = pl.BlockSpec((rows, span), lambda i: (0, i))
    return pl.pallas_call(
        attention_kernel,
        grid=(width // span,),
        in_specs=[by_cols] * 3
        + [pl.BlockSpec(piece.shape[:2] + (span,), lambda i: (0, 0, i)) for piece in pieces],
        out_specs=by_cols,
        out_shape=jax.ShapeDtypeStruct((rows, width), jnp.bfloat16),
        compiler_params=pltpu.CompilerParams(vmem_limit_bytes=VMEM_LIMIT),
        cost_estimate=pl.CostEstimate(
            flops=12 * rows * rows * width, bytes_accessed=12 * rows * width, transcendentals=0
        ),
        name="attention",
    )(queries, suffix_keys, suffix_values, *pieces)


def project_kernel(heads_ref, weight_ref, tokens_ref, gain_ref, attended_ref, normed_ref, held):
    step = pl.program_id(0)
    attended = jnp.dot(
        heads_ref[...], weight_ref[...], preferred_element_type=jnp.float32
    ).astype(jnp.bfloat16)
    attended_ref[...] = attended
    held[step] = tokens_ref[...].astype(jnp.float32) + attended.astype(jnp.float32)

    @pl.when(step == pl.num_programs(0) - 1)
    def finish():
        steps, rows, span = held.shape
        squares = jnp.zeros((rows, 1), jnp.float32)
        for piece in range(steps):
            part = held[piece]
            squares = squares + jnp.sum(part * part, axis=1, keepdims=True)
        factor = lax.rsqrt(squares / (steps * span) + 1e-06)
        for piece in range(steps):
            cols = slice(piece * span, (piece + 1) * span)
            normed_ref[:, cols] = (held[piece] * factor * gain_ref[:, cols]).astype(jnp.bfloat16)


def project(heads_out, out_weight, tokens, norm_gain):
    rows, width = tokens.shape
    span = 512
    steps = width // span
    by_cols = pl.BlockSpec((rows, span), lambda i: (0, i))
    return pl.pallas_call(
        project_kernel,
        grid=(steps,),
        in_specs=[
            pl.BlockSpec((rows, width), lambda i: (0, 0)),
            pl.BlockSpec((width, span), lambda i: (0, i)),
            by_cols,
            pl.BlockSpec((1, width), lambda i: (0, 0)),
        ],
        out_specs=[by_cols, pl.BlockSpec((rows, width), lambda i: (0, 0))],
        out_shape=[
            jax.ShapeDtypeStruct((rows, width), jnp.bfloat16),
            jax.ShapeDtypeStruct((rows, width), jnp.bfloat16),
        ],
        scratch_shapes=[pltpu.VMEM((steps, rows, span), jnp.float32)],
        compiler_params=pltpu.CompilerParams(vmem_limit_bytes=VMEM_LIMIT),
        cost_estimate=pl.CostEstimate(
            flops=2 * rows * width * width, bytes_accessed=2 * width * width, transcendentals=0
        ),
        name="project_and_norm",
    )(heads_out, out_weight, tokens, norm_gain.reshape(1, width))


def experts_kernel(capacity, count, slot_ref, gate_ref, *refs):
    rows_refs, refs = refs[:count], refs[count:]
    weight_refs, refs = refs[:4], refs[4:]
    out_refs, refs = refs[:count], refs[count:]
    picked, scaled, held, arrived = refs[0], refs[1], refs[2:6], refs[6]
    copies = [
        pltpu.make_async_copy(source, target, arrived.at[i])
        for i, (source, target) in enumerate(zip(weight_refs, held))
    ]
    for copy in copies:
        copy.start()
    rows = rows_refs[0].shape[0]
    hidden = held[1].shape[0]
    levels = lax.broadcasted_iota(jnp.int32, (2 * capacity, rows), 0)
    for one in range(count):
        chosen = (levels == slot_ref[one, 0]) | (levels == slot_ref[one, 1])
        taken = jnp.dot(
            chosen.astype(jnp.bfloat16), rows_refs[one][...], preferred_element_type=jnp.float32
        ).astype(jnp.bfloat16)
        picked[0, one * capacity : (one + 1) * capacity, :] = taken[:capacity]
        picked[1, one * capacity : (one + 1) * capacity, :] = taken[capacity:]
    for which in range(2):
        low = which * capacity
        copies[2 * which].wait()
        projected = jnp.dot(
            picked[which], held[2 * which][...], preferred_element_type=jnp.float32
        )
        gate = projected[:, :hidden]
        active = (gate / (1.0 + jnp.exp(-gate)) * projected[:, hidden:]).astype(jnp.bfloat16)
        copies[2 * which + 1].wait()
        result = jnp.dot(active, held[2 * which + 1][...], preferred_element_type=jnp.float32)
        for one in range(count):
            chosen = levels[low : low + capacity] == slot_ref[one, which]
            gates = jnp.sum(
                jnp.where(chosen, gate_ref[one, which], 0.0), axis=1, keepdims=True
            )
            scaled[one, low : low + capacity, :] = (
                result[one * capacity : (one + 1) * capacity, :] * gates
            ).astype(jnp.bfloat16)
    for one in range(count):
        chosen = (levels == slot_ref[one, 0]) | (levels == slot_ref[one, 1])
        out_refs[one][...] = lax.dot_general(
            chosen.astype(jnp.bfloat16),
            scaled[one],
            (((0,), (0,)), ((), ())),
            preferred_element_type=jnp.float32,
        ).astype(jnp.bfloat16)


def run_experts(blocks, slots, gates, weights, capacity):
    count = len(blocks)
    rows, width = blocks[0].shape
    hidden = weights[1].shape[0]
    total = 2 * count * capacity
    local = pl.BlockSpec(memory_space=pltpu.VMEM)
    return pl.pallas_call(
        lambda *refs: experts_kernel(capacity, count, *refs),
        in_specs=[local] * (2 + count) + [pl.BlockSpec(memory_space=pltpu.HBM)] * 4,
        out_specs=[local] * count,
        out_shape=[jax.ShapeDtypeStruct((rows, width), jnp.bfloat16)] * count,
        scratch_shapes=[
            pltpu.VMEM((2, count * capacity, width), jnp.bfloat16),
            pltpu.VMEM((count, 2 * capacity, width), jnp.bfloat16),
        ]
        + [pltpu.VMEM(one.shape, jnp.bfloat16) for one in weights]
        + [pltpu.SemaphoreType.DMA((4,))],
        compiler_params=pltpu.CompilerParams(vmem_limit_bytes=EXPERT_VMEM),
        cost_estimate=pl.CostEstimate(
            flops=total * width * hidden * 6,
            bytes_accessed=sum(one.size * 2 for one in weights) + count * rows * width * 4,
            transcendentals=total * hidden,
        ),
        name="experts",
    )(slots, gates, *blocks, *weights)


def half_expert(rows, gate_up, down_proj):
    hidden_units = down_proj.shape[0]
    projected = jnp.dot(rows, gate_up, preferred_element_type=jnp.float32)
    active = (jax.nn.silu(projected[:, :hidden_units]) * projected[:, hidden_units:]).astype(
        jnp.bfloat16
    )
    return jnp.dot(active, down_proj, preferred_element_type=jnp.float32).astype(jnp.bfloat16)


def exchange_plan(normed, routes, route_weights, gate_up, down, experts, capacity):
    rows_here, width = normed.shape
    flat_routes = routes.reshape(-1)
    onehot = (flat_routes[:, None] == jnp.arange(experts, dtype=jnp.int32)[None, :]).astype(
        jnp.int32
    )
    ranking = jnp.sum(jnp.cumsum(onehot, axis=0) * onehot, axis=1) - 1
    slots = flat_routes * capacity + ranking
    owners = jnp.arange(rows_here * TOP, dtype=jnp.int32) // TOP
    outgoing = jnp.zeros((experts * capacity, width), jnp.bfloat16).at[slots].set(normed[owners])
    buffer = jnp.broadcast_to(
        outgoing.reshape(experts, 1, capacity, width), (experts, 2, capacity, width)
    ).reshape(2 * experts, capacity, width)
    received = lax.all_to_all(buffer, ALL, split_axis=0, concat_axis=0, tiled=True)
    partial_rows = half_expert(received.reshape(-1, width), gate_up, down).reshape(
        2 * experts, capacity, width
    )
    returned = lax.all_to_all(partial_rows, ALL, split_axis=0, concat_axis=0, tiled=True)
    halves = returned.reshape(experts, 2, capacity, width)
    expert_table = lax.optimization_barrier(
        (halves[:, 0].astype(jnp.float32) + halves[:, 1].astype(jnp.float32)).astype(jnp.bfloat16)
    ).reshape(experts * capacity, width)
    picked = expert_table[slots].astype(jnp.float32)
    weighted_rows = picked * route_weights.reshape(-1)[:, None]
    return jnp.sum(weighted_rows.reshape(rows_here, TOP, width), axis=1).astype(jnp.bfloat16)


def own_slots(table, mine, first_slot):
    named = table[:, :TOP] == mine.astype(jnp.float32)
    gates = jnp.sum(jnp.where(named, table[:, TOP:], 0.0), axis=1)
    member = jnp.any(named, axis=1)
    rows = table.shape[-1]
    before = jnp.arange(rows)[:, None] <= jnp.arange(rows)[None, :]
    ranks = jnp.dot(
        member.astype(jnp.bfloat16),
        before.astype(jnp.bfloat16),
        preferred_element_type=jnp.float32,
    ).astype(jnp.int32)
    return jnp.where(member, ranks - 1 + first_slot, -1), gates


def swap(array, axis):
    return lax.ppermute(array, axis, [(0, 1), (1, 0)])


def shift(array, axis, amount):
    size = lax.axis_size(axis)
    return lax.ppermute(array, axis, [(i, (i + amount) % size) for i in range(size)])


def add(*arrays):
    return sum(one.astype(jnp.float32) for one in arrays).astype(jnp.bfloat16)


def along_line(block):
    columns = lax.axis_size("line")
    blocks = {0: block}
    for back in nearest_first()[1:]:
        if back <= columns // 2:
            blocks[back] = shift(blocks[back - 1], "line", 1)
        else:
            blocks[back] = shift(blocks[(back + 1) % columns], "line", -1)
    return [blocks[back] for back in range(columns)]


def nearest_first():
    columns = lax.axis_size("line")
    return sorted(range(columns), key=lambda back: (min(back, columns - back), back))


def prefix_pieces(kv, table, weights):
    order = nearest_first()
    held, swapped = {0: kv}, {}
    ready = [0]
    for i in range(1, len(order), 2):
        fresh = order[i : i + 2]
        for back in fresh:
            step = 1 if back <= len(order) // 2 else -1
            held[back] = shift(held[(back - step) % len(order)], "line", step)
        for back in ready:
            swapped[back] = swap(held[back], "side")
        moved, crossed, table, weights = lax.optimization_barrier(
            ([held[back] for back in fresh], [swapped[back] for back in ready], table, weights)
        )
        if i == 1:
            others = [swap(one, "core") for one in weights]
        held.update(zip(fresh, moved))
        swapped.update(zip(ready, crossed))
        ready = fresh
    for back in ready:
        swapped[back] = swap(held[back], "side")
    tables = [table] + [shift(table, "line", back) for back in range(1, len(order))]
    tables, crossed = lax.optimization_barrier((tables, [swapped[back] for back in ready]))
    swapped.update(zip(ready, crossed))
    return list(held.values()) + list(swapped.values()), jnp.stack(tables), others


def relative_slots(table, capacity):
    columns = lax.axis_size("line")
    far, core, line = lax.axis_index("far"), lax.axis_index("core"), lax.axis_index("line")
    table = table.reshape((4 * columns,) + table.shape[3:])
    own = (far * 2 + core) * columns + line
    other = (far * 2 + 1 - core) * columns + line
    own_slot, own_gate = own_slots(table, own, 0)
    other_slot, other_gate = own_slots(table, other, capacity)
    shape = (4, columns, 2, 1, -1)
    slots = jnp.stack([own_slot, other_slot], axis=1).reshape(shape)
    gates = jnp.stack([own_gate, other_gate], axis=1).reshape(shape)
    return slots, gates


def spread(normed):
    columns = lax.axis_size("line")
    beside, across = swap(normed, "side"), swap(normed, "far")
    planes = {0: [normed, beside, across, swap(beside, "far")]}
    up, down = shift(normed, "line", 1), shift(normed, "line", -1)
    lines = {1: up, columns - 1: down}
    for back in nearest_first()[3:]:
        step = 1 if back <= columns // 2 else -1
        lines[back] = shift(lines[back - step], "line", step)
        far_block = swap(lines[back], "far")
        planes[back] = [
            lines[back],
            swap(lines[back], "side"),
            far_block,
            swap(far_block, "side"),
        ]
    across_up, beside_down = shift(across, "line", 1), shift(beside, "line", -1)
    planes[1] = [up, swap(up, "side"), across_up, swap(across_up, "side")]
    planes[columns - 1] = [down, beside_down, swap(down, "far"), swap(beside_down, "far")]
    return planes


def gather_plan(normed, slots, gates, weights, capacity):
    columns = lax.axis_size("line")
    order = nearest_first()
    planes = spread(normed)
    results, first_corner, previous = {}, None, None
    for i, back in enumerate(order):
        mine = slots[:, back]
        if i > 0:
            mine, previous = lax.optimization_barrier((mine, previous))
            results[order[i - 1]] = previous
        if i == 2:
            first_corner = swap(results[1][3], "side")
        if i == len(order) - 1 and i > 2:
            mine, first_corner = lax.optimization_barrier((mine, first_corner))
        previous = run_experts(planes[back], mine, gates[:, back], weights, capacity)
    results[order[-1]] = previous
    here, beside, across, corner = results[1]
    up = add(here, swap(beside, "side"))
    across_up = add(across, first_corner)
    here, beside, across, corner = results[columns - 1]
    beside_down = add(beside, swap(corner, "far"))
    down = add(here, swap(across, "far"))
    parts = []
    for back in order[3:]:
        here, beside, across, corner = results[back]
        far_sum = add(across, swap(corner, "side"))
        total = add(here, swap(beside, "side"), swap(far_sum, "far"))
        parts.append(shift(total, "line", -back))
    here, beside, across, corner = results[0]
    across = add(across, shift(across_up, "line", -1))
    beside = add(beside, swap(corner, "far"), shift(beside_down, "line", 1))
    parts = parts + [shift(up, "line", -1), shift(down, "line", 1)]
    return add(here, swap(across, "far"), swap(beside, "side"), *parts)


def on_device(
    tokens,
    queries,
    suffix_keys,
    suffix_values,
    prefix_keys,
    prefix_values,
    out_weight,
    norm_gain,
    routes,
    route_weights,
    gate_up_weight,
    down_weight,
):
    rows_here, width = tokens.shape
    devices = lax.axis_size(ALL)
    experts = devices // 2
    capacity = 4 * rows_here * TOP // (3 * experts)
    gather_fits = (
        devices * rows_here * width * 2 <= GATHER_BUDGET and lax.axis_size("line") > 2
    )
    kv = jnp.concatenate([prefix_keys, prefix_values])
    weights = [gate_up_weight[0], down_weight[0]]
    if gather_fits:
        table = jnp.concatenate([routes.T.astype(jnp.float32), route_weights.T])
        pieces, table, others = prefix_pieces(kv, table, weights)
        beside = swap(table, "side")
    else:
        pieces = [lax.all_gather(kv, ("line", "side"), axis=1, tiled=True)]
    heads_out = attention(queries, suffix_keys, suffix_values, pieces)
    if gather_fits:
        heads_out, beside = lax.optimization_barrier((heads_out, beside))
        table = jnp.stack([table, beside])
        across = swap(table, "far")
    attended, normed = project(heads_out, out_weight, tokens, norm_gain)
    if gather_fits:
        normed, others, across = lax.optimization_barrier((normed, others, across))
        slots, gates = relative_slots(jnp.stack([table, across]), capacity)
        routed = gather_plan(normed, slots, gates, weights + others, capacity)
    else:
        routed = exchange_plan(
            normed, routes, route_weights, weights[0], weights[1], experts, capacity
        )
    return (attended, routed)


def solution(mesh):
    groups, members = mesh.shape["grp"], mesh.shape["dev"]
    fine = Mesh(mesh.devices.reshape(groups // 2, 2, members // 2, 2), ALL)
    rows = P(ALL, None)
    prefix = P(("far", "core"), ("line", "side"), None)
    stacked = P(ALL, None, None)
    return jax.shard_map(
        on_device,
        mesh=fine,
        in_specs=(rows,) * 4
        + (prefix, prefix, P(), P(), rows, rows, stacked, stacked),
        out_specs=(rows, rows),
        check_vma=False,
    )
```

```python
import math

import jax
import jax.numpy as jnp
from jax import lax
from jax.experimental import pallas as pl
from jax.experimental.pallas import tpu as pltpu
from jax.sharding import Mesh
from jax.sharding import PartitionSpec as P

HEADS = 16
HEAD_DIM = 128
TOP = 6
ALL = ("far", "core", "line", "side")
GATHER_BUDGET = 40 * 2**20
ATTEND_VMEM = 24 * 2**20
EXPERT_VMEM = 36 * 2**20


def attend_kernel(count, gain_ref, *refs):
    pieces, refs = refs[:count], refs[count:]
    sources, refs = refs[:5], refs[5:]
    attended_ref, normed_ref, heads, residual = refs[:4]
    held, arrived = refs[4:9], refs[9]
    copies = [
        pltpu.make_async_copy(source, target, arrived.at[i])
        for i, (source, target) in enumerate(zip(sources, held))
    ]
    for copy in copies:
        copy.start()
    q_ref, sk_ref, sv_ref, tokens_ref, weight_ref = held
    rows, width = heads.shape
    scale = 1.0 / math.sqrt(HEAD_DIM)
    causal = lax.broadcasted_iota(jnp.int32, (rows, rows), 0) >= lax.broadcasted_iota(
        jnp.int32, (rows, rows), 1
    )
    contract = (((1,), (1,)), ((), ()))
    for copy in copies[:3]:
        copy.wait()
    for head in range(width // HEAD_DIM):
        cols = slice(head * HEAD_DIM, (head + 1) * HEAD_DIM)
        query = q_ref[:, cols]
        keys = jnp.concatenate([piece[0, :, cols] for piece in pieces])
        values = jnp.concatenate([piece[1, :, cols] for piece in pieces])
        prefix = (
            lax.dot_general(query, keys, contract, preferred_element_type=jnp.float32) * scale
        )
        suffix = (
            lax.dot_general(query, sk_ref[:, cols], contract, preferred_element_type=jnp.float32)
            * scale
        )
        suffix = jnp.where(causal, suffix, -jnp.inf)
        top = jnp.maximum(
            jnp.max(prefix, axis=1, keepdims=True), jnp.max(suffix, axis=1, keepdims=True)
        )
        prefix = jnp.exp(prefix - top)
        suffix = jnp.exp(suffix - top)
        total = jnp.sum(prefix, axis=1, keepdims=True) + jnp.sum(suffix, axis=1, keepdims=True)
        mixed = jnp.dot(
            prefix.astype(jnp.bfloat16), values, preferred_element_type=jnp.float32
        ) + jnp.dot(
            suffix.astype(jnp.bfloat16), sv_ref[:, cols], preferred_element_type=jnp.float32
        )
        heads[:, cols] = (mixed / total).astype(jnp.bfloat16)
    for copy in copies[3:]:
        copy.wait()
    span = 512
    squares = jnp.zeros((rows, 1), jnp.float32)
    for low in range(0, width, span):
        cols = slice(low, low + span)
        attended = jnp.dot(
            heads[...], weight_ref[:, cols], preferred_element_type=jnp.float32
        ).astype(jnp.bfloat16)
        attended_ref[:, cols] = attended
        part = tokens_ref[:, cols].astype(jnp.float32) + attended.astype(jnp.float32)
        residual[:, cols] = part
        squares = squares + jnp.sum(part * part, axis=1, keepdims=True)
    factor = lax.rsqrt(squares / width + 1e-06)
    for low in range(0, width, span):
        cols = slice(low, low + span)
        normed_ref[:, cols] = (residual[:, cols] * factor * gain_ref[:, cols]).astype(
            jnp.bfloat16
        )


def attend(queries, suffix_keys, suffix_values, pieces, tokens, out_weight, norm_gain):
    rows, width = tokens.shape
    sources = [queries, suffix_keys, suffix_values, tokens, out_weight]
    local = pl.BlockSpec(memory_space=pltpu.VMEM)
    return pl.pallas_call(
        lambda *refs: attend_kernel(len(pieces), *refs),
        in_specs=[local] * (1 + len(pieces)) + [pl.BlockSpec(memory_space=pltpu.HBM)] * 5,
        out_specs=[local] * 2,
        out_shape=[jax.ShapeDtypeStruct((rows, width), jnp.bfloat16)] * 2,
        scratch_shapes=[
            pltpu.VMEM((rows, width), jnp.bfloat16),
            pltpu.VMEM((rows, width), jnp.float32),
        ]
        + [pltpu.VMEM(one.shape, jnp.bfloat16) for one in sources]
        + [pltpu.SemaphoreType.DMA((5,))],
        compiler_params=pltpu.CompilerParams(vmem_limit_bytes=ATTEND_VMEM),
        cost_estimate=pl.CostEstimate(
            flops=12 * rows * width * width, bytes_accessed=4 * rows * width, transcendentals=0
        ),
        name="attend_project_norm",
    )(norm_gain.reshape(1, width), *pieces, *sources)


def experts_kernel(capacity, count, slot_ref, gate_ref, *refs):
    rows_refs, refs = refs[:count], refs[count:]
    weight_refs, refs = refs[:4], refs[4:]
    out_refs, refs = refs[:count], refs[count:]
    picked, scaled, held, arrived = refs[0], refs[1], refs[2:6], refs[6]
    copies = [
        pltpu.make_async_copy(source, target, arrived.at[i])
        for i, (source, target) in enumerate(zip(weight_refs, held))
    ]
    for copy in copies:
        copy.start()
    rows = rows_refs[0].shape[0]
    hidden = held[1].shape[0]
    levels = lax.broadcasted_iota(jnp.int32, (2 * capacity, rows), 0)
    for one in range(count):
        chosen = (levels == slot_ref[one, 0]) | (levels == slot_ref[one, 1])
        taken = jnp.dot(
            chosen.astype(jnp.bfloat16), rows_refs[one][...], preferred_element_type=jnp.float32
        ).astype(jnp.bfloat16)
        picked[0, one * capacity : (one + 1) * capacity, :] = taken[:capacity]
        picked[1, one * capacity : (one + 1) * capacity, :] = taken[capacity:]
    for which in range(2):
        low = which * capacity
        copies[2 * which].wait()
        projected = jnp.dot(
            picked[which], held[2 * which][...], preferred_element_type=jnp.float32
        )
        gate = projected[:, :hidden]
        active = (gate / (1.0 + jnp.exp(-gate)) * projected[:, hidden:]).astype(jnp.bfloat16)
        copies[2 * which + 1].wait()
        result = jnp.dot(active, held[2 * which + 1][...], preferred_element_type=jnp.float32)
        for one in range(count):
            chosen = levels[low : low + capacity] == slot_ref[one, which]
            gates = jnp.sum(
                jnp.where(chosen, gate_ref[one, which], 0.0), axis=1, keepdims=True
            )
            scaled[one, low : low + capacity, :] = (
                result[one * capacity : (one + 1) * capacity, :] * gates
            ).astype(jnp.bfloat16)
    for one in range(count):
        chosen = (levels == slot_ref[one, 0]) | (levels == slot_ref[one, 1])
        out_refs[one][...] = lax.dot_general(
            chosen.astype(jnp.bfloat16),
            scaled[one],
            (((0,), (0,)), ((), ())),
            preferred_element_type=jnp.float32,
        ).astype(jnp.bfloat16)


def run_experts(blocks, slots, gates, weights, capacity):
    count = len(blocks)
    rows, width = blocks[0].shape
    hidden = weights[1].shape[0]
    total = 2 * count * capacity
    local = pl.BlockSpec(memory_space=pltpu.VMEM)
    return pl.pallas_call(
        lambda *refs: experts_kernel(capacity, count, *refs),
        in_specs=[local] * (2 + count) + [pl.BlockSpec(memory_space=pltpu.HBM)] * 4,
        out_specs=[local] * count,
        out_shape=[jax.ShapeDtypeStruct((rows, width), jnp.bfloat16)] * count,
        scratch_shapes=[
            pltpu.VMEM((2, count * capacity, width), jnp.bfloat16),
            pltpu.VMEM((count, 2 * capacity, width), jnp.bfloat16),
        ]
        + [pltpu.VMEM(one.shape, jnp.bfloat16) for one in weights]
        + [pltpu.SemaphoreType.DMA((4,))],
        compiler_params=pltpu.CompilerParams(vmem_limit_bytes=EXPERT_VMEM),
        cost_estimate=pl.CostEstimate(
            flops=total * width * hidden * 12,
            bytes_accessed=count * rows * width,
            transcendentals=total * hidden,
        ),
        name="experts",
    )(slots, gates, *blocks, *weights)


def half_expert(rows, gate_up, down_proj):
    hidden_units = down_proj.shape[0]
    projected = jnp.dot(rows, gate_up, preferred_element_type=jnp.float32)
    active = (jax.nn.silu(projected[:, :hidden_units]) * projected[:, hidden_units:]).astype(
        jnp.bfloat16
    )
    return jnp.dot(active, down_proj, preferred_element_type=jnp.float32).astype(jnp.bfloat16)


def exchange_plan(normed, routes, route_weights, gate_up, down, experts, capacity):
    rows_here, width = normed.shape
    flat_routes = routes.reshape(-1)
    onehot = (flat_routes[:, None] == jnp.arange(experts, dtype=jnp.int32)[None, :]).astype(
        jnp.int32
    )
    ranking = jnp.sum(jnp.cumsum(onehot, axis=0) * onehot, axis=1) - 1
    slots = flat_routes * capacity + ranking
    owners = jnp.arange(rows_here * TOP, dtype=jnp.int32) // TOP
    outgoing = jnp.zeros((experts * capacity, width), jnp.bfloat16).at[slots].set(normed[owners])
    buffer = jnp.broadcast_to(
        outgoing.reshape(experts, 1, capacity, width), (experts, 2, capacity, width)
    ).reshape(2 * experts, capacity, width)
    received = lax.all_to_all(buffer, ALL, split_axis=0, concat_axis=0, tiled=True)
    partial_rows = half_expert(received.reshape(-1, width), gate_up, down).reshape(
        2 * experts, capacity, width
    )
    returned = lax.all_to_all(partial_rows, ALL, split_axis=0, concat_axis=0, tiled=True)
    halves = returned.reshape(experts, 2, capacity, width)
    expert_table = lax.optimization_barrier(
        (halves[:, 0].astype(jnp.float32) + halves[:, 1].astype(jnp.float32)).astype(jnp.bfloat16)
    ).reshape(experts * capacity, width)
    picked = expert_table[slots].astype(jnp.float32)
    weighted_rows = picked * route_weights.reshape(-1)[:, None]
    return jnp.sum(weighted_rows.reshape(rows_here, TOP, width), axis=1).astype(jnp.bfloat16)


def own_slots(table, mine, first_slot):
    named = table[:, :TOP] == mine.astype(jnp.float32)
    gates = jnp.sum(jnp.where(named, table[:, TOP:], 0.0), axis=1)
    member = jnp.any(named, axis=1)
    rows = table.shape[-1]
    before = jnp.arange(rows)[:, None] <= jnp.arange(rows)[None, :]
    ranks = jnp.dot(
        member.astype(jnp.bfloat16),
        before.astype(jnp.bfloat16),
        preferred_element_type=jnp.float32,
    ).astype(jnp.int32)
    return jnp.where(member, ranks - 1 + first_slot, -1), gates


def swap(array, axis):
    return lax.ppermute(array, axis, [(0, 1), (1, 0)])


def shift(array, axis, amount):
    size = lax.axis_size(axis)
    return lax.ppermute(array, axis, [(i, (i + amount) % size) for i in range(size)])


def add(*arrays):
    return sum(one.astype(jnp.float32) for one in arrays).astype(jnp.bfloat16)


def along_line(block):
    columns = lax.axis_size("line")
    blocks = {0: block}
    for back in nearest_first()[1:]:
        if back <= columns // 2:
            blocks[back] = shift(blocks[back - 1], "line", 1)
        else:
            blocks[back] = shift(blocks[(back + 1) % columns], "line", -1)
    return [blocks[back] for back in range(columns)]


def nearest_first():
    columns = lax.axis_size("line")
    return sorted(range(columns), key=lambda back: (min(back, columns - back), back))


def prefix_pieces(kv, table, weights):
    order = nearest_first()
    held, swapped = {0: kv}, {}
    ready = [0]
    for i in range(1, len(order), 2):
        fresh = order[i : i + 2]
        for back in fresh:
            step = 1 if back <= len(order) // 2 else -1
            held[back] = shift(held[(back - step) % len(order)], "line", step)
        for back in ready:
            swapped[back] = swap(held[back], "side")
        if i == 1:
            tables = [table] + [shift(table, "line", back) for back in range(1, len(order))]
        moved, crossed, tables, weights = lax.optimization_barrier(
            ([held[back] for back in fresh], [swapped[back] for back in ready], tables, weights)
        )
        if i == 1:
            others = [swap(one, "core") for one in weights]
        held.update(zip(fresh, moved))
        swapped.update(zip(ready, crossed))
        ready = fresh
    for back in ready:
        swapped[back] = swap(held[back], "side")
    table = jnp.stack(tables)
    beside, crossed = lax.optimization_barrier(
        (swap(table, "side"), [swapped[back] for back in ready])
    )
    swapped.update(zip(ready, crossed))
    table = jnp.stack([table, beside])
    return list(held.values()) + list(swapped.values()), table, others


def relative_slots(table, capacity):
    columns = lax.axis_size("line")
    far, core, line = lax.axis_index("far"), lax.axis_index("core"), lax.axis_index("line")
    table = table.reshape((4 * columns,) + table.shape[3:])
    own = (far * 2 + core) * columns + line
    other = (far * 2 + 1 - core) * columns + line
    own_slot, own_gate = own_slots(table, own, 0)
    other_slot, other_gate = own_slots(table, other, capacity)
    shape = (4, columns, 2, 1, -1)
    slots = jnp.stack([own_slot, other_slot], axis=1).reshape(shape)
    gates = jnp.stack([own_gate, other_gate], axis=1).reshape(shape)
    return slots, gates


def spread(normed):
    columns = lax.axis_size("line")
    beside, across = swap(normed, "side"), swap(normed, "far")
    up, down = shift(normed, "line", 1), shift(normed, "line", -1)
    planes = {0: [normed, beside, across, swap(beside, "far")]}
    up, down, beside, across = lax.optimization_barrier((up, down, beside, across))
    lines = {1: up, columns - 1: down}
    for back in nearest_first()[3:]:
        step = 1 if back <= columns // 2 else -1
        lines[back] = shift(lines[back - step], "line", step)
        far_block = swap(lines[back], "far")
        planes[back] = [
            lines[back],
            swap(lines[back], "side"),
            far_block,
            swap(far_block, "side"),
        ]
    across_up, beside_down = shift(across, "line", 1), shift(beside, "line", -1)
    planes[1] = [up, swap(up, "side"), across_up, swap(across_up, "side")]
    planes[columns - 1] = [down, beside_down, swap(down, "far"), swap(beside_down, "far")]
    return planes


def gather_plan(normed, slots, gates, weights, capacity):
    columns = lax.axis_size("line")
    distant = nearest_first()[3:]
    order = [0, 1] + distant + [columns - 1]
    planes = spread(normed)
    results, corner_up, previous = {}, None, None
    for i, back in enumerate(order):
        mine = slots[:, back]
        if i > 0:
            mine, previous = lax.optimization_barrier((mine, previous))
            results[order[i - 1]] = previous
        if back == 1:
            mine, planes[columns - 1][:3] = lax.optimization_barrier(
                (mine, planes[columns - 1][:3])
            )
        if i == 2:
            corner_up = swap(results[1][3], "side")
            results[0], planes[back][3] = lax.optimization_barrier(
                (results[0], planes[back][3])
            )
        if i == 3:
            mine, corner_up = lax.optimization_barrier((mine, corner_up))
        previous = run_experts(planes[back], mine, gates[:, back], weights, capacity)
    results[order[-1]] = previous
    parts = []
    for back in distant:
        here, beside, across, corner = results[back]
        side_sum = add(beside, swap(corner, "far"))
        total = add(here, swap(across, "far"), swap(side_sum, "side"))
        parts.append(shift(total, "line", -back))
    here, beside, across, corner = results[1]
    up = add(here, swap(beside, "side"))
    across_up = add(across, corner_up)
    here, beside, across, corner = results[columns - 1]
    beside_down = add(beside, swap(corner, "far"))
    down = add(here, swap(across, "far"))
    here, beside, across, corner = results[0]
    across = add(across, swap(corner, "side"), shift(across_up, "line", -1))
    beside = add(beside, shift(beside_down, "line", 1))
    parts = parts + [shift(up, "line", -1), shift(down, "line", 1)]
    return add(here, swap(across, "far"), swap(beside, "side"), *parts)


def on_device(
    tokens,
    queries,
    suffix_keys,
    suffix_values,
    prefix_keys,
    prefix_values,
    out_weight,
    norm_gain,
    routes,
    route_weights,
    gate_up_weight,
    down_weight,
):
    rows_here, width = tokens.shape
    devices = lax.axis_size(ALL)
    experts = devices // 2
    capacity = 4 * rows_here * TOP // (3 * experts)
    gather_fits = (
        devices * rows_here * width * 2 <= GATHER_BUDGET and lax.axis_size("line") > 2
    )
    kv = jnp.concatenate([prefix_keys, prefix_values])
    weights = [gate_up_weight[0], down_weight[0]]
    if gather_fits:
        table = jnp.concatenate([routes.T.astype(jnp.float32), route_weights.T])
        pieces, table, others = prefix_pieces(kv, table, weights)
        across = swap(table, "far")
    else:
        pieces = [lax.all_gather(kv, ("line", "side"), axis=1, tiled=True)]
    attended, normed = attend(
        queries, suffix_keys, suffix_values, pieces, tokens, out_weight, norm_gain
    )
    if gather_fits:
        normed, others, across = lax.optimization_barrier((normed, others, across))
        slots, gates = relative_slots(jnp.stack([table, across]), capacity)
        routed = gather_plan(normed, slots, gates, weights + others, capacity)
    else:
        routed = exchange_plan(
            normed, routes, route_weights, weights[0], weights[1], experts, capacity
        )
    return (attended, routed)


def solution(mesh):
    groups, members = mesh.shape["grp"], mesh.shape["dev"]
    fine = Mesh(mesh.devices.reshape(groups // 2, 2, members // 2, 2), ALL)
    rows = P(ALL, None)
    prefix = P(("far", "core"), ("line", "side"), None)
    stacked = P(ALL, None, None)
    return jax.shard_map(
        on_device,
        mesh=fine,
        in_specs=(rows,) * 4
        + (prefix, prefix, P(), P(), rows, rows, stacked, stacked),
        out_specs=(rows, rows),
        check_vma=False,
    )
```

```python
import math

import jax
import jax.numpy as jnp
from jax import lax
from jax.experimental import pallas as pl
from jax.experimental.pallas import tpu as pltpu
from jax.sharding import Mesh
from jax.sharding import PartitionSpec as P

HEADS = 16
HEAD_DIM = 128
TOP = 6
ALL = ("far", "core", "line", "side")
GATHER_BUDGET = 40 * 2**20
ATTEND_VMEM = 52 * 2**20
EXPERT_VMEM = 40 * 2**20


def attend_kernel(count, gain_ref, *refs):
    pieces, refs = refs[:count], refs[count:]
    sources, refs = refs[:5], refs[5:]
    attended_ref, normed_ref, heads, residual = refs[:4]
    held, arrived = refs[4:9], refs[9]
    copies = [
        pltpu.make_async_copy(source, target, arrived.at[i])
        for i, (source, target) in enumerate(zip(sources, held))
    ]
    for copy in copies:
        copy.start()
    q_ref, sk_ref, sv_ref, tokens_ref, weight_ref = held
    rows, width = heads.shape
    scale = 1.0 / math.sqrt(HEAD_DIM)
    causal = lax.broadcasted_iota(jnp.int32, (rows, rows), 0) >= lax.broadcasted_iota(
        jnp.int32, (rows, rows), 1
    )
    contract = (((1,), (1,)), ((), ()))
    for copy in copies[:3]:
        copy.wait()
    for head in range(width // HEAD_DIM):
        cols = slice(head * HEAD_DIM, (head + 1) * HEAD_DIM)
        query = q_ref[:, cols]
        keys = jnp.concatenate([piece[0, :, cols] for piece in pieces])
        values = jnp.concatenate([piece[1, :, cols] for piece in pieces])
        prefix = (
            lax.dot_general(query, keys, contract, preferred_element_type=jnp.float32) * scale
        )
        suffix = (
            lax.dot_general(query, sk_ref[:, cols], contract, preferred_element_type=jnp.float32)
            * scale
        )
        suffix = jnp.where(causal, suffix, -jnp.inf)
        top = jnp.maximum(
            jnp.max(prefix, axis=1, keepdims=True), jnp.max(suffix, axis=1, keepdims=True)
        )
        prefix = jnp.exp(prefix - top)
        suffix = jnp.exp(suffix - top)
        total = jnp.sum(prefix, axis=1, keepdims=True) + jnp.sum(suffix, axis=1, keepdims=True)
        mixed = jnp.dot(
            prefix.astype(jnp.bfloat16), values, preferred_element_type=jnp.float32
        ) + jnp.dot(
            suffix.astype(jnp.bfloat16), sv_ref[:, cols], preferred_element_type=jnp.float32
        )
        heads[:, cols] = (mixed / total).astype(jnp.bfloat16)
    for copy in copies[3:]:
        copy.wait()
    span = 512
    squares = jnp.zeros((rows, 1), jnp.float32)
    for low in range(0, width, span):
        cols = slice(low, low + span)
        attended = jnp.dot(
            heads[...], weight_ref[:, cols], preferred_element_type=jnp.float32
        ).astype(jnp.bfloat16)
        attended_ref[:, cols] = attended
        part = tokens_ref[:, cols].astype(jnp.float32) + attended.astype(jnp.float32)
        residual[:, cols] = part
        squares = squares + jnp.sum(part * part, axis=1, keepdims=True)
    factor = lax.rsqrt(squares / width + 1e-06)
    for low in range(0, width, span):
        cols = slice(low, low + span)
        normed_ref[:, cols] = (residual[:, cols] * factor * gain_ref[:, cols]).astype(
            jnp.bfloat16
        )


def attend(queries, suffix_keys, suffix_values, pieces, tokens, out_weight, norm_gain):
    rows, width = tokens.shape
    sources = [queries, suffix_keys, suffix_values, tokens, out_weight]
    local = pl.BlockSpec(memory_space=pltpu.VMEM)
    return pl.pallas_call(
        lambda *refs: attend_kernel(len(pieces), *refs),
        in_specs=[local] * (1 + len(pieces)) + [pl.BlockSpec(memory_space=pltpu.HBM)] * 5,
        out_specs=[local] * 2,
        out_shape=[jax.ShapeDtypeStruct((rows, width), jnp.bfloat16)] * 2,
        scratch_shapes=[
            pltpu.VMEM((rows, width), jnp.bfloat16),
            pltpu.VMEM((rows, width), jnp.float32),
        ]
        + [pltpu.VMEM(one.shape, jnp.bfloat16) for one in sources]
        + [pltpu.SemaphoreType.DMA((5,))],
        compiler_params=pltpu.CompilerParams(vmem_limit_bytes=ATTEND_VMEM),
        cost_estimate=pl.CostEstimate(
            flops=12 * rows * width * width, bytes_accessed=4 * rows * width, transcendentals=0
        ),
        name="attend_project_norm",
    )(norm_gain.reshape(1, width), *pieces, *sources)


def experts_kernel(capacity, count, slot_ref, gate_ref, *refs):
    rows_refs, refs = refs[:count], refs[count:]
    weight_refs, refs = refs[:4], refs[4:]
    out_refs, refs = refs[:count], refs[count:]
    picked, scaled, held, landed, arrived = refs[0], refs[1], refs[2:6], refs[6], refs[7]
    loads = [
        pltpu.make_async_copy(rows_refs[i], landed.at[i], arrived.at[4 + i])
        for i in range(count)
    ]
    copies = [
        pltpu.make_async_copy(source, target, arrived.at[i])
        for i, (source, target) in enumerate(zip(weight_refs, held))
    ]
    for copy in loads + copies:
        copy.start()
    rows = landed.shape[1]
    hidden = held[1].shape[0]
    levels = lax.broadcasted_iota(jnp.int32, (2 * capacity, rows), 0)
    for one in range(count):
        chosen = (levels == slot_ref[one, 0]) | (levels == slot_ref[one, 1])
        loads[one].wait()
        taken = jnp.dot(
            chosen.astype(jnp.bfloat16), landed[one], preferred_element_type=jnp.float32
        ).astype(jnp.bfloat16)
        picked[0, one * capacity : (one + 1) * capacity, :] = taken[:capacity]
        picked[1, one * capacity : (one + 1) * capacity, :] = taken[capacity:]
    for which in range(2):
        low = which * capacity
        copies[2 * which].wait()
        projected = jnp.dot(
            picked[which], held[2 * which][...], preferred_element_type=jnp.float32
        )
        gate = projected[:, :hidden]
        active = (gate / (1.0 + jnp.exp(-gate)) * projected[:, hidden:]).astype(jnp.bfloat16)
        copies[2 * which + 1].wait()
        result = jnp.dot(active, held[2 * which + 1][...], preferred_element_type=jnp.float32)
        for one in range(count):
            chosen = levels[low : low + capacity] == slot_ref[one, which]
            gates = jnp.sum(
                jnp.where(chosen, gate_ref[one, which], 0.0), axis=1, keepdims=True
            )
            scaled[one, low : low + capacity, :] = (
                result[one * capacity : (one + 1) * capacity, :] * gates
            ).astype(jnp.bfloat16)
    for one in range(count):
        chosen = (levels == slot_ref[one, 0]) | (levels == slot_ref[one, 1])
        out_refs[one][...] = lax.dot_general(
            chosen.astype(jnp.bfloat16),
            scaled[one],
            (((0,), (0,)), ((), ())),
            preferred_element_type=jnp.float32,
        ).astype(jnp.bfloat16)


def run_experts(blocks, slots, gates, weights, capacity):
    count = len(blocks)
    rows, width = blocks[0].shape
    hidden = weights[1].shape[0]
    total = 2 * count * capacity
    local = pl.BlockSpec(memory_space=pltpu.VMEM)
    return pl.pallas_call(
        lambda *refs: experts_kernel(capacity, count, *refs),
        in_specs=[local] * 2 + [pl.BlockSpec(memory_space=pltpu.HBM)] * (count + 4),
        out_specs=[local] * count,
        out_shape=[jax.ShapeDtypeStruct((rows, width), jnp.bfloat16)] * count,
        scratch_shapes=[
            pltpu.VMEM((2, count * capacity, width), jnp.bfloat16),
            pltpu.VMEM((count, 2 * capacity, width), jnp.bfloat16),
        ]
        + [pltpu.VMEM(one.shape, jnp.bfloat16) for one in weights]
        + [
            pltpu.VMEM((count, rows, width), jnp.bfloat16),
            pltpu.SemaphoreType.DMA((4 + count,)),
        ],
        compiler_params=pltpu.CompilerParams(vmem_limit_bytes=EXPERT_VMEM),
        cost_estimate=pl.CostEstimate(
            flops=total * width * hidden * 12,
            bytes_accessed=count * rows * width,
            transcendentals=total * hidden,
        ),
        name="experts",
    )(slots, gates, *blocks, *weights)


def half_expert(rows, gate_up, down_proj):
    hidden_units = down_proj.shape[0]
    projected = jnp.dot(rows, gate_up, preferred_element_type=jnp.float32)
    active = (jax.nn.silu(projected[:, :hidden_units]) * projected[:, hidden_units:]).astype(
        jnp.bfloat16
    )
    return jnp.dot(active, down_proj, preferred_element_type=jnp.float32).astype(jnp.bfloat16)


def exchange_plan(normed, routes, route_weights, gate_up, down, experts, capacity):
    rows_here, width = normed.shape
    flat_routes = routes.reshape(-1)
    onehot = (flat_routes[:, None] == jnp.arange(experts, dtype=jnp.int32)[None, :]).astype(
        jnp.int32
    )
    ranking = jnp.sum(jnp.cumsum(onehot, axis=0) * onehot, axis=1) - 1
    slots = flat_routes * capacity + ranking
    owners = jnp.arange(rows_here * TOP, dtype=jnp.int32) // TOP
    outgoing = jnp.zeros((experts * capacity, width), jnp.bfloat16).at[slots].set(normed[owners])
    buffer = jnp.broadcast_to(
        outgoing.reshape(experts, 1, capacity, width), (experts, 2, capacity, width)
    ).reshape(2 * experts, capacity, width)
    received = lax.all_to_all(buffer, ALL, split_axis=0, concat_axis=0, tiled=True)
    partial_rows = half_expert(received.reshape(-1, width), gate_up, down).reshape(
        2 * experts, capacity, width
    )
    returned = lax.all_to_all(partial_rows, ALL, split_axis=0, concat_axis=0, tiled=True)
    halves = returned.reshape(experts, 2, capacity, width)
    expert_table = lax.optimization_barrier(
        (halves[:, 0].astype(jnp.float32) + halves[:, 1].astype(jnp.float32)).astype(jnp.bfloat16)
    ).reshape(experts * capacity, width)
    picked = expert_table[slots].astype(jnp.float32)
    weighted_rows = picked * route_weights.reshape(-1)[:, None]
    return jnp.sum(weighted_rows.reshape(rows_here, TOP, width), axis=1).astype(jnp.bfloat16)


def own_slots(table, mine, first_slot):
    named = table[:, :TOP] == mine.astype(jnp.float32)
    gates = jnp.sum(jnp.where(named, table[:, TOP:], 0.0), axis=1)
    member = jnp.any(named, axis=1)
    rows = table.shape[-1]
    before = jnp.arange(rows)[:, None] <= jnp.arange(rows)[None, :]
    ranks = jnp.dot(
        member.astype(jnp.bfloat16),
        before.astype(jnp.bfloat16),
        preferred_element_type=jnp.float32,
    ).astype(jnp.int32)
    return jnp.where(member, ranks - 1 + first_slot, -1), gates


def swap(array, axis):
    return lax.ppermute(array, axis, [(0, 1), (1, 0)])


def shift(array, axis, amount):
    size = lax.axis_size(axis)
    return lax.ppermute(array, axis, [(i, (i + amount) % size) for i in range(size)])


def add(*arrays):
    return sum(one.astype(jnp.float32) for one in arrays).astype(jnp.bfloat16)


def along_line(block):
    columns = lax.axis_size("line")
    blocks = {0: block}
    for back in nearest_first()[1:]:
        if back <= columns // 2:
            blocks[back] = shift(blocks[back - 1], "line", 1)
        else:
            blocks[back] = shift(blocks[(back + 1) % columns], "line", -1)
    return [blocks[back] for back in range(columns)]


def nearest_first():
    columns = lax.axis_size("line")
    return sorted(range(columns), key=lambda back: (min(back, columns - back), back))


def prefix_pieces(kv, table, weights):
    order = nearest_first()
    held, swapped = {0: kv}, {}
    ready = [0]
    for i in range(1, len(order), 2):
        fresh = order[i : i + 2]
        for back in fresh:
            step = 1 if back <= len(order) // 2 else -1
            held[back] = shift(held[(back - step) % len(order)], "line", step)
        for back in ready:
            swapped[back] = swap(held[back], "side")
        moved, crossed, table, weights = lax.optimization_barrier(
            ([held[back] for back in fresh], [swapped[back] for back in ready], table, weights)
        )
        if i == 1:
            others = [swap(one, "core") for one in weights]
        held.update(zip(fresh, moved))
        swapped.update(zip(ready, crossed))
        ready = fresh
    for back in ready:
        swapped[back] = swap(held[back], "side")
    tables = [table] + [shift(table, "line", back) for back in range(1, len(order))]
    tables, crossed = lax.optimization_barrier((tables, [swapped[back] for back in ready]))
    swapped.update(zip(ready, crossed))
    return list(held.values()) + list(swapped.values()), jnp.stack(tables), others


def relative_slots(table, capacity):
    columns = lax.axis_size("line")
    far, core, line = lax.axis_index("far"), lax.axis_index("core"), lax.axis_index("line")
    table = table.reshape((4 * columns,) + table.shape[3:])
    own = (far * 2 + core) * columns + line
    other = (far * 2 + 1 - core) * columns + line
    own_slot, own_gate = own_slots(table, own, 0)
    other_slot, other_gate = own_slots(table, other, capacity)
    shape = (4, columns, 2, 1, -1)
    slots = jnp.stack([own_slot, other_slot], axis=1).reshape(shape)
    gates = jnp.stack([own_gate, other_gate], axis=1).reshape(shape)
    return slots, gates


def over_plane(block, axes):
    first = swap(block, axes[0])
    second = swap(block, axes[1])
    corner = swap(first, axes[1])
    if axes[0] == "side":
        return [block, first, second, corner]
    return [block, second, first, corner]


def gather_plan(normed, slots, gates, weights, capacity):
    order = nearest_first()
    blocks = along_line(normed)
    axes = [("side", "far") if i % 2 == 0 else ("far", "side") for i in range(len(order))]
    results, corner = [], None
    for i in range(0, len(order), 2):
        group = order[i : i + 2]
        planes = []
        for j, back in enumerate(group):
            planes = planes + over_plane(blocks[back], axes[i + j])
        mine = jnp.concatenate([slots[:, back] for back in group])
        share = jnp.concatenate([gates[:, back] for back in group])
        if i == 2:
            corner = swap(results[1][3], axes[1][0])
        if i > 0:
            mine, corner, results[-1] = lax.optimization_barrier((mine, corner, results[-1]))
        outputs = run_experts(planes, mine, share, weights, capacity)
        for j in range(len(group)):
            results.append(list(outputs[4 * j : 4 * j + 4]))
    parts = []
    for i, back in enumerate(order):
        here, beside, across, last = results[i]
        near, rest = (beside, across) if axes[i][0] == "side" else (across, beside)
        moved = corner if i == 1 else swap(last, axes[i][0])
        total = add(here, swap(near, axes[i][0]), swap(add(rest, moved), axes[i][1]))
        parts.append(shift(total, "line", -back) if back else total)
    return add(*parts)


def on_device(
    tokens,
    queries,
    suffix_keys,
    suffix_values,
    prefix_keys,
    prefix_values,
    out_weight,
    norm_gain,
    routes,
    route_weights,
    gate_up_weight,
    down_weight,
):
    rows_here, width = tokens.shape
    devices = lax.axis_size(ALL)
    experts = devices // 2
    capacity = 4 * rows_here * TOP // (3 * experts)
    gather_fits = devices * rows_here * width * 2 <= GATHER_BUDGET
    kv = jnp.concatenate([prefix_keys, prefix_values])
    weights = [gate_up_weight[0], down_weight[0]]
    if gather_fits:
        table = jnp.concatenate([routes.T.astype(jnp.float32), route_weights.T])
        pieces, table, others = prefix_pieces(kv, table, weights)
        beside = swap(table, "side")
    else:
        pieces = [lax.all_gather(kv, ("line", "side"), axis=1, tiled=True)]
    attended, normed = attend(
        queries, suffix_keys, suffix_values, pieces, tokens, out_weight, norm_gain
    )
    if gather_fits:
        normed, others, beside = lax.optimization_barrier((normed, others, beside))
        table = jnp.stack([table, beside])
        across = swap(table, "far")
        slots, gates = relative_slots(jnp.stack([table, across]), capacity)
        routed = gather_plan(normed, slots, gates, weights + others, capacity)
    else:
        routed = exchange_plan(
            normed, routes, route_weights, weights[0], weights[1], experts, capacity
        )
    return (attended, routed)


def solution(mesh):
    groups, members = mesh.shape["grp"], mesh.shape["dev"]
    fine = Mesh(mesh.devices.reshape(groups // 2, 2, members // 2, 2), ALL)
    rows = P(ALL, None)
    prefix = P(("far", "core"), ("line", "side"), None)
    stacked = P(ALL, None, None)
    return jax.shard_map(
        on_device,
        mesh=fine,
        in_specs=(rows,) * 4
        + (prefix, prefix, P(), P(), rows, rows, stacked, stacked),
        out_specs=(rows, rows),
        check_vma=False,
    )
```

```python
import math

import jax
import jax.numpy as jnp
from jax import lax
from jax.experimental import pallas as pl
from jax.experimental.pallas import tpu as pltpu
from jax.sharding import Mesh
from jax.sharding import PartitionSpec as P

HEADS = 16
HEAD_DIM = 128
TOP = 6
ALL = ("far", "core", "line", "side")
GATHER_BUDGET = 40 * 2**20
ATTEND_VMEM = 52 * 2**20
EXPERT_VMEM = 40 * 2**20


def attend_kernel(count, gain_ref, *refs):
    pieces, refs = refs[:count], refs[count:]
    sources, refs = refs[:5], refs[5:]
    attended_ref, normed_ref, heads, residual = refs[:4]
    held, arrived = refs[4:9], refs[9]
    copies = [
        pltpu.make_async_copy(source, target, arrived.at[i])
        for i, (source, target) in enumerate(zip(sources, held))
    ]
    for copy in copies:
        copy.start()
    q_ref, sk_ref, sv_ref, tokens_ref, weight_ref = held
    rows, width = heads.shape
    scale = 1.0 / math.sqrt(HEAD_DIM)
    causal = lax.broadcasted_iota(jnp.int32, (rows, rows), 0) >= lax.broadcasted_iota(
        jnp.int32, (rows, rows), 1
    )
    contract = (((1,), (1,)), ((), ()))
    for copy in copies[:3]:
        copy.wait()
    for head in range(width // HEAD_DIM):
        cols = slice(head * HEAD_DIM, (head + 1) * HEAD_DIM)
        query = q_ref[:, cols]
        keys = jnp.concatenate([piece[0, :, cols] for piece in pieces])
        values = jnp.concatenate([piece[1, :, cols] for piece in pieces])
        prefix = (
            lax.dot_general(query, keys, contract, preferred_element_type=jnp.float32) * scale
        )
        suffix = (
            lax.dot_general(query, sk_ref[:, cols], contract, preferred_element_type=jnp.float32)
            * scale
        )
        suffix = jnp.where(causal, suffix, -jnp.inf)
        top = jnp.maximum(
            jnp.max(prefix, axis=1, keepdims=True), jnp.max(suffix, axis=1, keepdims=True)
        )
        prefix = jnp.exp(prefix - top)
        suffix = jnp.exp(suffix - top)
        total = jnp.sum(prefix, axis=1, keepdims=True) + jnp.sum(suffix, axis=1, keepdims=True)
        mixed = jnp.dot(
            prefix.astype(jnp.bfloat16), values, preferred_element_type=jnp.float32
        ) + jnp.dot(
            suffix.astype(jnp.bfloat16), sv_ref[:, cols], preferred_element_type=jnp.float32
        )
        heads[:, cols] = (mixed / total).astype(jnp.bfloat16)
    for copy in copies[3:]:
        copy.wait()
    span = 512
    squares = jnp.zeros((rows, 1), jnp.float32)
    for low in range(0, width, span):
        cols = slice(low, low + span)
        attended = jnp.dot(
            heads[...], weight_ref[:, cols], preferred_element_type=jnp.float32
        ).astype(jnp.bfloat16)
        attended_ref[:, cols] = attended
        part = tokens_ref[:, cols].astype(jnp.float32) + attended.astype(jnp.float32)
        residual[:, cols] = part
        squares = squares + jnp.sum(part * part, axis=1, keepdims=True)
    factor = lax.rsqrt(squares / width + 1e-06)
    for low in range(0, width, span):
        cols = slice(low, low + span)
        normed_ref[:, cols] = (residual[:, cols] * factor * gain_ref[:, cols]).astype(
            jnp.bfloat16
        )


def attend(queries, suffix_keys, suffix_values, pieces, tokens, out_weight, norm_gain):
    rows, width = tokens.shape
    sources = [queries, suffix_keys, suffix_values, tokens, out_weight]
    local = pl.BlockSpec(memory_space=pltpu.VMEM)
    return pl.pallas_call(
        lambda *refs: attend_kernel(len(pieces), *refs),
        in_specs=[local] * (1 + len(pieces)) + [pl.BlockSpec(memory_space=pltpu.HBM)] * 5,
        out_specs=[local] * 2,
        out_shape=[jax.ShapeDtypeStruct((rows, width), jnp.bfloat16)] * 2,
        scratch_shapes=[
            pltpu.VMEM((rows, width), jnp.bfloat16),
            pltpu.VMEM((rows, width), jnp.float32),
        ]
        + [pltpu.VMEM(one.shape, jnp.bfloat16) for one in sources]
        + [pltpu.SemaphoreType.DMA((5,))],
        compiler_params=pltpu.CompilerParams(vmem_limit_bytes=ATTEND_VMEM),
        cost_estimate=pl.CostEstimate(
            flops=12 * rows * width * width, bytes_accessed=4 * rows * width, transcendentals=0
        ),
        name="attend_project_norm",
    )(norm_gain.reshape(1, width), *pieces, *sources)


def experts_kernel(capacity, count, slot_ref, gate_ref, *refs):
    rows_refs, refs = refs[:count], refs[count:]
    weight_refs, refs = refs[:4], refs[4:]
    out_refs, refs = refs[:count], refs[count:]
    picked, scaled, held, landed, arrived = refs[0], refs[1], refs[2:6], refs[6], refs[7]
    loads = [
        pltpu.make_async_copy(rows_refs[i], landed.at[i], arrived.at[4 + i])
        for i in range(count)
    ]
    copies = [
        pltpu.make_async_copy(source, target, arrived.at[i])
        for i, (source, target) in enumerate(zip(weight_refs, held))
    ]
    for copy in loads + copies:
        copy.start()
    rows = landed.shape[1]
    hidden = held[1].shape[0]
    levels = lax.broadcasted_iota(jnp.int32, (2 * capacity, rows), 0)
    for one in range(count):
        chosen = (levels == slot_ref[one, 0]) | (levels == slot_ref[one, 1])
        loads[one].wait()
        taken = jnp.dot(
            chosen.astype(jnp.bfloat16), landed[one], preferred_element_type=jnp.float32
        ).astype(jnp.bfloat16)
        picked[0, one * capacity : (one + 1) * capacity, :] = taken[:capacity]
        picked[1, one * capacity : (one + 1) * capacity, :] = taken[capacity:]
    for which in range(2):
        low = which * capacity
        copies[2 * which].wait()
        projected = jnp.dot(
            picked[which], held[2 * which][...], preferred_element_type=jnp.float32
        )
        gate = projected[:, :hidden]
        active = (gate / (1.0 + jnp.exp(-gate)) * projected[:, hidden:]).astype(jnp.bfloat16)
        copies[2 * which + 1].wait()
        result = jnp.dot(active, held[2 * which + 1][...], preferred_element_type=jnp.float32)
        for one in range(count):
            chosen = levels[low : low + capacity] == slot_ref[one, which]
            gates = jnp.sum(
                jnp.where(chosen, gate_ref[one, which], 0.0), axis=1, keepdims=True
            )
            scaled[one, low : low + capacity, :] = (
                result[one * capacity : (one + 1) * capacity, :] * gates
            ).astype(jnp.bfloat16)
    for one in range(count):
        chosen = (levels == slot_ref[one, 0]) | (levels == slot_ref[one, 1])
        out_refs[one][...] = lax.dot_general(
            chosen.astype(jnp.bfloat16),
            scaled[one],
            (((0,), (0,)), ((), ())),
            preferred_element_type=jnp.float32,
        ).astype(jnp.bfloat16)


def run_experts(blocks, slots, gates, weights, capacity):
    count = len(blocks)
    rows, width = blocks[0].shape
    hidden = weights[1].shape[0]
    total = 2 * count * capacity
    local = pl.BlockSpec(memory_space=pltpu.VMEM)
    return pl.pallas_call(
        lambda *refs: experts_kernel(capacity, count, *refs),
        in_specs=[local] * 2 + [pl.BlockSpec(memory_space=pltpu.HBM)] * (count + 4),
        out_specs=[local] * count,
        out_shape=[jax.ShapeDtypeStruct((rows, width), jnp.bfloat16)] * count,
        scratch_shapes=[
            pltpu.VMEM((2, count * capacity, width), jnp.bfloat16),
            pltpu.VMEM((count, 2 * capacity, width), jnp.bfloat16),
        ]
        + [pltpu.VMEM(one.shape, jnp.bfloat16) for one in weights]
        + [
            pltpu.VMEM((count, rows, width), jnp.bfloat16),
            pltpu.SemaphoreType.DMA((4 + count,)),
        ],
        compiler_params=pltpu.CompilerParams(vmem_limit_bytes=EXPERT_VMEM),
        cost_estimate=pl.CostEstimate(
            flops=total * width * hidden * 12,
            bytes_accessed=count * rows * width,
            transcendentals=total * hidden,
        ),
        name="experts",
    )(slots, gates, *blocks, *weights)


def half_expert(rows, gate_up, down_proj):
    hidden_units = down_proj.shape[0]
    projected = jnp.dot(rows, gate_up, preferred_element_type=jnp.float32)
    active = (jax.nn.silu(projected[:, :hidden_units]) * projected[:, hidden_units:]).astype(
        jnp.bfloat16
    )
    return jnp.dot(active, down_proj, preferred_element_type=jnp.float32).astype(jnp.bfloat16)


def exchange_plan(normed, routes, route_weights, gate_up, down, experts, capacity):
    rows_here, width = normed.shape
    flat_routes = routes.reshape(-1)
    onehot = (flat_routes[:, None] == jnp.arange(experts, dtype=jnp.int32)[None, :]).astype(
        jnp.int32
    )
    ranking = jnp.sum(jnp.cumsum(onehot, axis=0) * onehot, axis=1) - 1
    slots = flat_routes * capacity + ranking
    owners = jnp.arange(rows_here * TOP, dtype=jnp.int32) // TOP
    outgoing = jnp.zeros((experts * capacity, width), jnp.bfloat16).at[slots].set(normed[owners])
    buffer = jnp.broadcast_to(
        outgoing.reshape(experts, 1, capacity, width), (experts, 2, capacity, width)
    ).reshape(2 * experts, capacity, width)
    received = lax.all_to_all(buffer, ALL, split_axis=0, concat_axis=0, tiled=True)
    partial_rows = half_expert(received.reshape(-1, width), gate_up, down).reshape(
        2 * experts, capacity, width
    )
    returned = lax.all_to_all(partial_rows, ALL, split_axis=0, concat_axis=0, tiled=True)
    halves = returned.reshape(experts, 2, capacity, width)
    expert_table = lax.optimization_barrier(
        (halves[:, 0].astype(jnp.float32) + halves[:, 1].astype(jnp.float32)).astype(jnp.bfloat16)
    ).reshape(experts * capacity, width)
    picked = expert_table[slots].astype(jnp.float32)
    weighted_rows = picked * route_weights.reshape(-1)[:, None]
    return jnp.sum(weighted_rows.reshape(rows_here, TOP, width), axis=1).astype(jnp.bfloat16)


def own_slots(table, mine, first_slot):
    named = table[:, :TOP] == mine.astype(jnp.float32)
    gates = jnp.sum(jnp.where(named, table[:, TOP:], 0.0), axis=1)
    member = jnp.any(named, axis=1)
    rows = table.shape[-1]
    before = jnp.arange(rows)[:, None] <= jnp.arange(rows)[None, :]
    ranks = jnp.dot(
        member.astype(jnp.bfloat16),
        before.astype(jnp.bfloat16),
        preferred_element_type=jnp.float32,
    ).astype(jnp.int32)
    return jnp.where(member, ranks - 1 + first_slot, -1), gates


def swap(array, axis):
    return lax.ppermute(array, axis, [(0, 1), (1, 0)])


def shift(array, axis, amount):
    size = lax.axis_size(axis)
    return lax.ppermute(array, axis, [(i, (i + amount) % size) for i in range(size)])


def add(*arrays):
    return sum(one.astype(jnp.float32) for one in arrays).astype(jnp.bfloat16)


def along_line(block):
    columns = lax.axis_size("line")
    blocks = {0: block}
    for back in nearest_first()[1:]:
        if back <= columns // 2:
            blocks[back] = shift(blocks[back - 1], "line", 1)
        else:
            blocks[back] = shift(blocks[(back + 1) % columns], "line", -1)
    return [blocks[back] for back in range(columns)]


def nearest_first():
    columns = lax.axis_size("line")
    return sorted(range(columns), key=lambda back: (min(back, columns - back), back))


def prefix_pieces(kv, table, weights):
    order = nearest_first()
    held, swapped = {0: kv}, {}
    ready = [0]
    for i in range(1, len(order), 2):
        fresh = order[i : i + 2]
        for back in fresh:
            step = 1 if back <= len(order) // 2 else -1
            held[back] = shift(held[(back - step) % len(order)], "line", step)
        for back in ready:
            swapped[back] = swap(held[back], "side")
        moved, crossed, table, weights = lax.optimization_barrier(
            ([held[back] for back in fresh], [swapped[back] for back in ready], table, weights)
        )
        if i == 1:
            others = [swap(one, "core") for one in weights]
        held.update(zip(fresh, moved))
        swapped.update(zip(ready, crossed))
        ready = fresh
    for back in ready:
        swapped[back] = swap(held[back], "side")
    tables = [table] + [shift(table, "line", back) for back in range(1, len(order))]
    tables, crossed = lax.optimization_barrier((tables, [swapped[back] for back in ready]))
    swapped.update(zip(ready, crossed))
    return list(held.values()) + list(swapped.values()), jnp.stack(tables), others


def relative_slots(table, capacity):
    columns = lax.axis_size("line")
    far, core, line = lax.axis_index("far"), lax.axis_index("core"), lax.axis_index("line")
    table = table.reshape((4 * columns,) + table.shape[3:])
    own = (far * 2 + core) * columns + line
    other = (far * 2 + 1 - core) * columns + line
    own_slot, own_gate = own_slots(table, own, 0)
    other_slot, other_gate = own_slots(table, other, capacity)
    shape = (4, columns, 2, 1, -1)
    slots = jnp.stack([own_slot, other_slot], axis=1).reshape(shape)
    gates = jnp.stack([own_gate, other_gate], axis=1).reshape(shape)
    return slots, gates


def over_plane(block, axes):
    first = swap(block, axes[0])
    second = swap(block, axes[1])
    corner = swap(first, axes[1])
    if axes[0] == "side":
        return [block, first, second, corner]
    return [block, second, first, corner]


def meet_early(results, corner, axes):
    _, beside, across, _ = results
    near, rest = (beside, across) if axes[0] == "side" else (across, beside)
    return swap(near, axes[0]), swap(add(rest, corner), axes[1])


def gather_plan(normed, slots, gates, weights, capacity):
    order = nearest_first()
    blocks = along_line(normed)
    axes = [("side", "far") if i % 2 == 0 else ("far", "side") for i in range(len(order))]
    results, corner = [], None
    for i in range(0, len(order), 2):
        group = order[i : i + 2]
        planes = []
        for j, back in enumerate(group):
            planes = planes + over_plane(blocks[back], axes[i + j])
        mine = jnp.concatenate([slots[:, back] for back in group])
        share = jnp.concatenate([gates[:, back] for back in group])
        if i == 2:
            corner = swap(results[1][3], axes[1][0])
        if i > 0:
            mine, corner, results[-1] = lax.optimization_barrier((mine, corner, results[-1]))
        if i == 2:
            early = meet_early(results[1], corner, axes[1])
        outputs = run_experts(planes, mine, share, weights, capacity)
        if i == 2:
            outputs, early = lax.optimization_barrier((outputs, early))
        for j in range(len(group)):
            results.append(list(outputs[4 * j : 4 * j + 4]))
    parts = {}
    parts[1] = add(results[1][0], *early)
    for i, back in reversed(list(enumerate(order))):
        if back == 1:
            continue
        here, beside, across, last = results[i]
        near, rest = (beside, across) if axes[i][0] == "side" else (across, beside)
        rest = add(rest, swap(last, axes[i][0]))
        if back == 0 and len(order) // 2 in parts:
            rest, parts[len(order) // 2] = lax.optimization_barrier(
                (rest, parts[len(order) // 2])
            )
        parts[back] = add(here, swap(near, axes[i][0]), swap(rest, axes[i][1]))
    columns = len(order)
    for back in range(columns // 2, 1, -1):
        parts[back - 1] = add(parts[back - 1], shift(parts[back], "line", -1))
    for back in range(columns // 2 + 1, columns - 1):
        parts[back + 1] = add(parts[back + 1], shift(parts[back], "line", 1))
    return add(parts[0], shift(parts[1], "line", -1), shift(parts[columns - 1], "line", 1))


def on_device(
    tokens,
    queries,
    suffix_keys,
    suffix_values,
    prefix_keys,
    prefix_values,
    out_weight,
    norm_gain,
    routes,
    route_weights,
    gate_up_weight,
    down_weight,
):
    rows_here, width = tokens.shape
    devices = lax.axis_size(ALL)
    experts = devices // 2
    capacity = 4 * rows_here * TOP // (3 * experts)
    gather_fits = devices * rows_here * width * 2 <= GATHER_BUDGET
    kv = jnp.concatenate([prefix_keys, prefix_values])
    weights = [gate_up_weight[0], down_weight[0]]
    if gather_fits:
        table = jnp.concatenate([routes.T.astype(jnp.float32), route_weights.T])
        pieces, table, others = prefix_pieces(kv, table, weights)
        beside = swap(table, "side")
    else:
        pieces = [lax.all_gather(kv, ("line", "side"), axis=1, tiled=True)]
    attended, normed = attend(
        queries, suffix_keys, suffix_values, pieces, tokens, out_weight, norm_gain
    )
    if gather_fits:
        normed, others, beside = lax.optimization_barrier((normed, others, beside))
        table = jnp.stack([table, beside])
        across = swap(table, "far")
        slots, gates = relative_slots(jnp.stack([table, across]), capacity)
        routed = gather_plan(normed, slots, gates, weights + others, capacity)
    else:
        routed = exchange_plan(
            normed, routes, route_weights, weights[0], weights[1], experts, capacity
        )
    return (attended, routed)


def solution(mesh):
    groups, members = mesh.shape["grp"], mesh.shape["dev"]
    fine = Mesh(mesh.devices.reshape(groups // 2, 2, members // 2, 2), ALL)
    rows = P(ALL, None)
    prefix = P(("far", "core"), ("line", "side"), None)
    stacked = P(ALL, None, None)
    return jax.shard_map(
        on_device,
        mesh=fine,
        in_specs=(rows,) * 4
        + (prefix, prefix, P(), P(), rows, rows, stacked, stacked),
        out_specs=(rows, rows),
        check_vma=False,
    )
```

```python
import math

import jax
import jax.numpy as jnp
from jax import lax
from jax.experimental import pallas as pl
from jax.experimental.pallas import tpu as pltpu
from jax.sharding import Mesh
from jax.sharding import PartitionSpec as P

HEADS = 16
HEAD_DIM = 128
TOP = 6
ALL = ("far", "core", "line", "side")
GATHER_BUDGET = 40 * 2**20
ATTEND_VMEM = 52 * 2**20
EXPERT_VMEM = 40 * 2**20


def attend_kernel(count, gain_ref, *refs):
    pieces, refs = refs[:count], refs[count:]
    sources, refs = refs[:5], refs[5:]
    attended_ref, normed_ref, heads, residual = refs[:4]
    held, arrived = refs[4:9], refs[9]
    copies = [
        pltpu.make_async_copy(source, target, arrived.at[i])
        for i, (source, target) in enumerate(zip(sources, held))
    ]
    for copy in copies:
        copy.start()
    q_ref, sk_ref, sv_ref, tokens_ref, weight_ref = held
    rows, width = heads.shape
    scale = 1.0 / math.sqrt(HEAD_DIM)
    causal = lax.broadcasted_iota(jnp.int32, (rows, rows), 0) >= lax.broadcasted_iota(
        jnp.int32, (rows, rows), 1
    )
    contract = (((1,), (1,)), ((), ()))
    for copy in copies[:3]:
        copy.wait()
    for head in range(width // HEAD_DIM):
        cols = slice(head * HEAD_DIM, (head + 1) * HEAD_DIM)
        query = q_ref[:, cols]
        keys = jnp.concatenate([piece[0, :, cols] for piece in pieces])
        values = jnp.concatenate([piece[1, :, cols] for piece in pieces])
        prefix = (
            lax.dot_general(query, keys, contract, preferred_element_type=jnp.float32) * scale
        )
        suffix = (
            lax.dot_general(query, sk_ref[:, cols], contract, preferred_element_type=jnp.float32)
            * scale
        )
        suffix = jnp.where(causal, suffix, -jnp.inf)
        top = jnp.maximum(
            jnp.max(prefix, axis=1, keepdims=True), jnp.max(suffix, axis=1, keepdims=True)
        )
        prefix = jnp.exp(prefix - top)
        suffix = jnp.exp(suffix - top)
        total = jnp.sum(prefix, axis=1, keepdims=True) + jnp.sum(suffix, axis=1, keepdims=True)
        mixed = jnp.dot(
            prefix.astype(jnp.bfloat16), values, preferred_element_type=jnp.float32
        ) + jnp.dot(
            suffix.astype(jnp.bfloat16), sv_ref[:, cols], preferred_element_type=jnp.float32
        )
        heads[:, cols] = (mixed / total).astype(jnp.bfloat16)
    for copy in copies[3:]:
        copy.wait()
    span = 512
    squares = jnp.zeros((rows, 1), jnp.float32)
    for low in range(0, width, span):
        cols = slice(low, low + span)
        attended = jnp.dot(
            heads[...], weight_ref[:, cols], preferred_element_type=jnp.float32
        ).astype(jnp.bfloat16)
        attended_ref[:, cols] = attended
        part = tokens_ref[:, cols].astype(jnp.float32) + attended.astype(jnp.float32)
        residual[:, cols] = part
        squares = squares + jnp.sum(part * part, axis=1, keepdims=True)
    factor = lax.rsqrt(squares / width + 1e-06)
    for low in range(0, width, span):
        cols = slice(low, low + span)
        normed_ref[:, cols] = (residual[:, cols] * factor * gain_ref[:, cols]).astype(
            jnp.bfloat16
        )


def attend(queries, suffix_keys, suffix_values, pieces, tokens, out_weight, norm_gain):
    rows, width = tokens.shape
    sources = [queries, suffix_keys, suffix_values, tokens, out_weight]
    local = pl.BlockSpec(memory_space=pltpu.VMEM)
    return pl.pallas_call(
        lambda *refs: attend_kernel(len(pieces), *refs),
        in_specs=[local] * (1 + len(pieces)) + [pl.BlockSpec(memory_space=pltpu.HBM)] * 5,
        out_specs=[local] * 2,
        out_shape=[jax.ShapeDtypeStruct((rows, width), jnp.bfloat16)] * 2,
        scratch_shapes=[
            pltpu.VMEM((rows, width), jnp.bfloat16),
            pltpu.VMEM((rows, width), jnp.float32),
        ]
        + [pltpu.VMEM(one.shape, jnp.bfloat16) for one in sources]
        + [pltpu.SemaphoreType.DMA((5,))],
        compiler_params=pltpu.CompilerParams(vmem_limit_bytes=ATTEND_VMEM),
        cost_estimate=pl.CostEstimate(
            flops=12 * rows * width * width, bytes_accessed=4 * rows * width, transcendentals=0
        ),
        name="attend_project_norm",
    )(norm_gain.reshape(1, width), *pieces, *sources)


def experts_kernel(capacity, count, slot_ref, gate_ref, *refs):
    rows_refs, refs = refs[:count], refs[count:]
    weight_refs, refs = refs[:4], refs[4:]
    out_refs, refs = refs[:count], refs[count:]
    picked, scaled, held, landed, arrived = refs[0], refs[1], refs[2:6], refs[6], refs[7]
    loads = [
        pltpu.make_async_copy(rows_refs[i], landed.at[i], arrived.at[4 + i])
        for i in range(count)
    ]
    copies = [
        pltpu.make_async_copy(source, target, arrived.at[i])
        for i, (source, target) in enumerate(zip(weight_refs, held))
    ]
    for copy in loads + copies:
        copy.start()
    rows = landed.shape[1]
    hidden = held[1].shape[0]
    levels = lax.broadcasted_iota(jnp.int32, (2 * capacity, rows), 0)
    for one in range(count):
        chosen = (levels == slot_ref[one, 0]) | (levels == slot_ref[one, 1])
        loads[one].wait()
        taken = jnp.dot(
            chosen.astype(jnp.bfloat16), landed[one], preferred_element_type=jnp.float32
        ).astype(jnp.bfloat16)
        picked[0, one * capacity : (one + 1) * capacity, :] = taken[:capacity]
        picked[1, one * capacity : (one + 1) * capacity, :] = taken[capacity:]
    for which in range(2):
        low = which * capacity
        copies[2 * which].wait()
        projected = jnp.dot(
            picked[which], held[2 * which][...], preferred_element_type=jnp.float32
        )
        gate = projected[:, :hidden]
        active = (gate / (1.0 + jnp.exp(-gate)) * projected[:, hidden:]).astype(jnp.bfloat16)
        copies[2 * which + 1].wait()
        result = jnp.dot(active, held[2 * which + 1][...], preferred_element_type=jnp.float32)
        for one in range(count):
            chosen = levels[low : low + capacity] == slot_ref[one, which]
            gates = jnp.sum(
                jnp.where(chosen, gate_ref[one, which], 0.0), axis=1, keepdims=True
            )
            scaled[one, low : low + capacity, :] = (
                result[one * capacity : (one + 1) * capacity, :] * gates
            ).astype(jnp.bfloat16)
    for one in range(count):
        chosen = (levels == slot_ref[one, 0]) | (levels == slot_ref[one, 1])
        out_refs[one][...] = lax.dot_general(
            chosen.astype(jnp.bfloat16),
            scaled[one],
            (((0,), (0,)), ((), ())),
            preferred_element_type=jnp.float32,
        ).astype(jnp.bfloat16)


def run_experts(blocks, slots, gates, weights, capacity):
    count = len(blocks)
    rows, width = blocks[0].shape
    hidden = weights[1].shape[0]
    total = 2 * count * capacity
    local = pl.BlockSpec(memory_space=pltpu.VMEM)
    return pl.pallas_call(
        lambda *refs: experts_kernel(capacity, count, *refs),
        in_specs=[local] * 2 + [pl.BlockSpec(memory_space=pltpu.HBM)] * (count + 4),
        out_specs=[local] * count,
        out_shape=[jax.ShapeDtypeStruct((rows, width), jnp.bfloat16)] * count,
        scratch_shapes=[
            pltpu.VMEM((2, count * capacity, width), jnp.bfloat16),
            pltpu.VMEM((count, 2 * capacity, width), jnp.bfloat16),
        ]
        + [pltpu.VMEM(one.shape, jnp.bfloat16) for one in weights]
        + [
            pltpu.VMEM((count, rows, width), jnp.bfloat16),
            pltpu.SemaphoreType.DMA((4 + count,)),
        ],
        compiler_params=pltpu.CompilerParams(vmem_limit_bytes=EXPERT_VMEM),
        cost_estimate=pl.CostEstimate(
            flops=total * width * hidden * 12,
            bytes_accessed=count * rows * width,
            transcendentals=total * hidden,
        ),
        name="experts",
    )(slots, gates, *blocks, *weights)


def half_expert(rows, gate_up, down_proj):
    hidden_units = down_proj.shape[0]
    projected = jnp.dot(rows, gate_up, preferred_element_type=jnp.float32)
    active = (jax.nn.silu(projected[:, :hidden_units]) * projected[:, hidden_units:]).astype(
        jnp.bfloat16
    )
    return jnp.dot(active, down_proj, preferred_element_type=jnp.float32).astype(jnp.bfloat16)


def exchange_plan(normed, routes, route_weights, gate_up, down, experts, capacity):
    rows_here, width = normed.shape
    flat_routes = routes.reshape(-1)
    onehot = (flat_routes[:, None] == jnp.arange(experts, dtype=jnp.int32)[None, :]).astype(
        jnp.int32
    )
    ranking = jnp.sum(jnp.cumsum(onehot, axis=0) * onehot, axis=1) - 1
    slots = flat_routes * capacity + ranking
    owners = jnp.arange(rows_here * TOP, dtype=jnp.int32) // TOP
    outgoing = jnp.zeros((experts * capacity, width), jnp.bfloat16).at[slots].set(normed[owners])
    buffer = jnp.broadcast_to(
        outgoing.reshape(experts, 1, capacity, width), (experts, 2, capacity, width)
    ).reshape(2 * experts, capacity, width)
    received = lax.all_to_all(buffer, ALL, split_axis=0, concat_axis=0, tiled=True)
    partial_rows = half_expert(received.reshape(-1, width), gate_up, down).reshape(
        2 * experts, capacity, width
    )
    returned = lax.all_to_all(partial_rows, ALL, split_axis=0, concat_axis=0, tiled=True)
    halves = returned.reshape(experts, 2, capacity, width)
    expert_table = lax.optimization_barrier(
        (halves[:, 0].astype(jnp.float32) + halves[:, 1].astype(jnp.float32)).astype(jnp.bfloat16)
    ).reshape(experts * capacity, width)
    picked = expert_table[slots].astype(jnp.float32)
    weighted_rows = picked * route_weights.reshape(-1)[:, None]
    return jnp.sum(weighted_rows.reshape(rows_here, TOP, width), axis=1).astype(jnp.bfloat16)


def own_slots(table, mine, first_slot):
    named = table[:, :TOP] == mine.astype(jnp.float32)
    gates = jnp.sum(jnp.where(named, table[:, TOP:], 0.0), axis=1)
    member = jnp.any(named, axis=1)
    rows = table.shape[-1]
    before = jnp.arange(rows)[:, None] <= jnp.arange(rows)[None, :]
    ranks = jnp.dot(
        member.astype(jnp.bfloat16),
        before.astype(jnp.bfloat16),
        preferred_element_type=jnp.float32,
    ).astype(jnp.int32)
    return jnp.where(member, ranks - 1 + first_slot, -1), gates


def swap(array, axis):
    return lax.ppermute(array, axis, [(0, 1), (1, 0)])


def shift(array, axis, amount):
    size = lax.axis_size(axis)
    return lax.ppermute(array, axis, [(i, (i + amount) % size) for i in range(size)])


def add(*arrays):
    return sum(one.astype(jnp.float32) for one in arrays).astype(jnp.bfloat16)


def along_line(block):
    columns = lax.axis_size("line")
    blocks = {0: block}
    for back in nearest_first()[1:]:
        if back <= columns // 2:
            blocks[back] = shift(blocks[back - 1], "line", 1)
        else:
            blocks[back] = shift(blocks[(back + 1) % columns], "line", -1)
    return [blocks[back] for back in range(columns)]


def nearest_first():
    columns = lax.axis_size("line")
    return sorted(range(columns), key=lambda back: (min(back, columns - back), back))


def prefix_pieces(kv, table, weights):
    order = nearest_first()
    held, swapped = {0: kv}, {}
    ready = [0]
    for i in range(1, len(order), 2):
        fresh = order[i : i + 2]
        for back in fresh:
            step = 1 if back <= len(order) // 2 else -1
            held[back] = shift(held[(back - step) % len(order)], "line", step)
        for back in ready:
            swapped[back] = swap(held[back], "side")
        moved, crossed, table, weights = lax.optimization_barrier(
            ([held[back] for back in fresh], [swapped[back] for back in ready], table, weights)
        )
        if i == 1:
            others = [swap(one, "core") for one in weights]
        held.update(zip(fresh, moved))
        swapped.update(zip(ready, crossed))
        ready = fresh
    for back in ready:
        swapped[back] = swap(held[back], "side")
    tables = [table] + [shift(table, "line", back) for back in range(1, len(order))]
    tables, crossed = lax.optimization_barrier((tables, [swapped[back] for back in ready]))
    swapped.update(zip(ready, crossed))
    return list(held.values()) + list(swapped.values()), jnp.stack(tables), others


def relative_slots(table, capacity):
    columns = lax.axis_size("line")
    far, core, line = lax.axis_index("far"), lax.axis_index("core"), lax.axis_index("line")
    table = table.reshape((4 * columns,) + table.shape[3:])
    own = (far * 2 + core) * columns + line
    other = (far * 2 + 1 - core) * columns + line
    own_slot, own_gate = own_slots(table, own, 0)
    other_slot, other_gate = own_slots(table, other, capacity)
    shape = (4, columns, 2, 1, -1)
    slots = jnp.stack([own_slot, other_slot], axis=1).reshape(shape)
    gates = jnp.stack([own_gate, other_gate], axis=1).reshape(shape)
    return slots, gates


def over_plane(block, axes):
    first = swap(block, axes[0])
    second = swap(block, axes[1])
    corner = swap(first, axes[1])
    if axes[0] == "side":
        return [block, first, second, corner]
    return [block, second, first, corner]


def first_two(results, axes):
    _, beside, across, last = results
    near = beside if axes[0] == "side" else across
    return swap(near, axes[0]), swap(last, axes[0])


def gather_plan(normed, slots, gates, weights, capacity):
    order = nearest_first()
    blocks = along_line(normed)
    axes = [("side", "far") if i % 2 == 0 else ("far", "side") for i in range(len(order))]
    results, early = [], []
    for i in range(0, len(order), 2):
        group = order[i : i + 2]
        planes = [over_plane(blocks[back], axes[i + j]) for j, back in enumerate(group)]
        mine = jnp.concatenate([slots[:, back] for back in group])
        share = jnp.concatenate([gates[:, back] for back in group])
        if i > 0:
            direct = [one[1:3] for one in planes]
            results, direct = lax.optimization_barrier((results, direct))
            planes = [one[:1] + two + one[3:] for one, two in zip(planes, direct)]
            results, planes, mine = lax.optimization_barrier((results, planes, mine))
            early = early + [first_two(results[j], axes[j]) for j in range(i - 2, i)]
        outputs = run_experts(sum(planes, []), mine, share, weights, capacity)
        if i > 0:
            outputs, early = lax.optimization_barrier((outputs, early))
        for j in range(len(group)):
            results.append(list(outputs[4 * j : 4 * j + 4]))
    parts = {}
    for i, back in reversed(list(enumerate(order))):
        here, beside, across, _ = results[i]
        rest = across if axes[i][0] == "side" else beside
        near, moved = early[i] if i < len(early) else first_two(results[i], axes[i])
        rest = add(rest, moved)
        if back == 0 and len(order) // 2 in parts:
            rest, parts[len(order) // 2] = lax.optimization_barrier(
                (rest, parts[len(order) // 2])
            )
        parts[back] = add(here, near, swap(rest, axes[i][1]))
    columns = len(order)
    for back in range(columns // 2, 1, -1):
        parts[back - 1] = add(parts[back - 1], shift(parts[back], "line", -1))
    for back in range(columns // 2 + 1, columns - 1):
        parts[back + 1] = add(parts[back + 1], shift(parts[back], "line", 1))
    return add(parts[0], shift(parts[1], "line", -1), shift(parts[columns - 1], "line", 1))


def on_device(
    tokens,
    queries,
    suffix_keys,
    suffix_values,
    prefix_keys,
    prefix_values,
    out_weight,
    norm_gain,
    routes,
    route_weights,
    gate_up_weight,
    down_weight,
):
    rows_here, width = tokens.shape
    devices = lax.axis_size(ALL)
    experts = devices // 2
    capacity = 4 * rows_here * TOP // (3 * experts)
    gather_fits = devices * rows_here * width * 2 <= GATHER_BUDGET
    kv = jnp.concatenate([prefix_keys, prefix_values])
    weights = [gate_up_weight[0], down_weight[0]]
    if gather_fits:
        table = jnp.concatenate([routes.T.astype(jnp.float32), route_weights.T])
        pieces, table, others = prefix_pieces(kv, table, weights)
        beside = swap(table, "side")
    else:
        pieces = [lax.all_gather(kv, ("line", "side"), axis=1, tiled=True)]
    attended, normed = attend(
        queries, suffix_keys, suffix_values, pieces, tokens, out_weight, norm_gain
    )
    if gather_fits:
        normed, others, beside = lax.optimization_barrier((normed, others, beside))
        table = jnp.stack([table, beside])
        across = swap(table, "far")
        slots, gates = relative_slots(jnp.stack([table, across]), capacity)
        routed = gather_plan(normed, slots, gates, weights + others, capacity)
    else:
        routed = exchange_plan(
            normed, routes, route_weights, weights[0], weights[1], experts, capacity
        )
    return (attended, routed)


def solution(mesh):
    groups, members = mesh.shape["grp"], mesh.shape["dev"]
    fine = Mesh(mesh.devices.reshape(groups // 2, 2, members // 2, 2), ALL)
    rows = P(ALL, None)
    prefix = P(("far", "core"), ("line", "side"), None)
    stacked = P(ALL, None, None)
    return jax.shard_map(
        on_device,
        mesh=fine,
        in_specs=(rows,) * 4
        + (prefix, prefix, P(), P(), rows, rows, stacked, stacked),
        out_specs=(rows, rows),
        check_vma=False,
    )
```
